256 devices in a mesh: gx: 8 (over z_lo, x), gy: 8 (over y, core), gz: 4 (over z_hi).
Axes of the slice: x: 4, y: 4, z: 8 (z_hi: 4, z_lo: 2; z = z_hi * 2 + z_lo), core: 2. Of those that a mesh axis runs over, the one named last changes fastest.
Arguments:
- displacements: float32 [3, 16, 16, 128], P(None, 'gx', 'gy', 'gz'), may hold values from -0.3 to 0.3
- species: int32 [16, 16, 128], P('gx', 'gy', 'gz'), may hold values from 0 to 2
- neighbor_index: int32 [32, 16, 16, 128], P(None, 'gx', 'gy', 'gz'), may hold values from 0 to 543, as said below
- probes: float32 [8, 3, 16, 16, 128], P(None, None, 'gx', 'gy', 'gz'), may hold values from -4 to 4
- embedding: float32 [3, 128], replicated, may hold values from -5 to 5
- w_radial1: float32 [8, 64], replicated, may hold values from -2 to 2
- w_radial2: float32 [64, 128], replicated, may hold values from -0.75 to 0.75
- w_node: float32 [128, 128], replicated, may hold values from -0.5 to 0.5
- readout: float32 [128], replicated, may hold values from -0.5 to 0.5
- spectral_radius: float32 [1], replicated, may hold values from 0.15 to 0.4
Outputs:
- chebyshev: float32 [2, 8, 3, 16, 16, 128], P(None, None, None, 'gx', 'gy', 'gz')
- moments: float32 [4, 8], replicated
The draws below stay inside these ranges and needn't reach their ends.
Inputs may be any that keep to these rules, and one draw needn't show every extreme that they name: `neighbor_index`: entry n of atom a is the row-major flat index, in a block of (4) x (4) x (34) sites formed by a's domain and one layer of adjacent sites around it, either of a lattice site adjacent to a (differing by -1, 0 or 1 in each coordinate, not a itself) or of a itself for an empty slot; no adjacent site appears twice in one list.
All inputs are finite; a program needn't handle non-finite values.
Results may differ from the reference program's by a relative error of at most 0.0003.
Values sent between devices are 32-bit elements; how exact they have to be, the bound alone decides.
A program may use at most 192 MiB of HBM per device.

```python
import math
import jax
import jax.numpy as jnp
from jax import lax

CX = 2
CY = 2
CZ = 32
C = 128
RHIDDEN = 64
RADIAL = 8
SPECIES = 3
NEIGH = 32
PROBES = 8
STEPS = 3
NX = 16
NY = 16
NZ = 128


def draw_neighbor_index(key, part):
    key = jax.random.fold_in(key, 11)
    keep_key = jax.random.fold_in(key, 1)
    order_key = jax.random.fold_in(key, 2)
    code_list = jnp.concatenate([jnp.arange(13, dtype=jnp.int32), jnp.arange(14, 27, dtype=jnp.int32)])
    forced = (code_list == 0) | (code_list == 26)
    keep = jax.random.randint(keep_key, (26, NX, NY, NZ), 0, 8) != 0
    keep = keep | forced[:, None, None, None]
    scores = jax.random.randint(order_key, (26, NX, NY, NZ), 0, 1048576) * 32 + jnp.arange(26, dtype=jnp.int32)[:, None, None, None]
    order = jnp.argsort(scores, axis=0)
    chosen = jnp.where(keep, code_list[:, None, None, None], 13)
    permuted = jnp.take_along_axis(chosen, order, axis=0)
    slot_codes = jnp.concatenate([permuted, jnp.full((NEIGH - 26, NX, NY, NZ), 13, jnp.int32)], 0)
    shape = slot_codes.shape
    local_x = lax.broadcasted_iota(jnp.int32, shape, 1) % CX
    local_y = lax.broadcasted_iota(jnp.int32, shape, 2) % CY
    local_z = lax.broadcasted_iota(jnp.int32, shape, 3) % CZ
    site_x = local_x + 1 + slot_codes // 9 - 1
    site_y = local_y + 1 + slot_codes // 3 % 3 - 1
    site_z = local_z + 1 + slot_codes % 3 - 1
    return (site_x * (CY + 2) * (CZ + 2) + site_y * (CZ + 2) + site_z).astype(jnp.int32)


def with_ends(values, own_key, low, largest):
    extent = values.shape
    place = [jax.random.randint(jax.random.fold_in(own_key, axis), (), 0, extent[axis]) for axis in range(len(extent))]
    values = values.at[tuple(place)].set(low)
    longest = extent.index(max(extent))
    place[longest] = (place[longest] + 1) % extent[longest]
    return values.at[tuple(place)].set(largest)


def steps_of(rng, shape, pieces, smallest, high):
    def one(axis_at, blocks):
        steps = jax.random.uniform(jax.random.fold_in(jax.random.fold_in(rng, 6), axis_at), (blocks,), jnp.float32, smallest / len(pieces), high / len(pieces))
        return jnp.repeat(jnp.exp(steps), shape[axis_at] // blocks).reshape((-1,) + (1,) * (len(shape) - axis_at - 1))

    loudness = one(*pieces[0])
    for cut in pieces[1:]:
        loudness = loudness * one(*cut)
    return loudness


def normal_values(rng, dims, width, bound, split=(), kind=jnp.bfloat16):
    values = width * jax.random.normal(rng, dims, jnp.float32)
    if split:
        values = values * steps_of(rng, dims, split, -0.22, 0.18)
    return jnp.clip(values, -bound, bound).astype(kind)


def setup_inputs(seed: int = 0) -> dict:
    splits = jax.random.split(jax.random.key(seed), 11)
    return {
        "displacements": jnp.clip(jax.random.uniform(splits[0], (3, NX, NY, NZ), jnp.float32, -0.3, 0.3) * steps_of(splits[0], (3, NX, NY, NZ), ((1, 8), (2, 8), (3, 4)), -0.4, 0.0), -0.3, 0.3),
        "species": with_ends(jax.random.randint(splits[1], (NX, NY, NZ), 0, SPECIES), jax.random.fold_in(splits[1], 1), 0, SPECIES - 1).astype(jnp.int32),
        "neighbor_index": draw_neighbor_index(jax.random.fold_in(splits[10], 71), 0),
        "probes": normal_values(splits[3], (PROBES, 3, NX, NY, NZ), 1.0, 4.0, ((2, 8), (3, 8), (4, 4)), jnp.float32),
        "embedding": normal_values(splits[4], (SPECIES, C), 1.0, 5.0, (), jnp.float32),
        "w_radial1": normal_values(splits[5], (RADIAL, RHIDDEN), RADIAL ** -0.5, 2.0, (), jnp.float32),
        "w_radial2": normal_values(splits[6], (RHIDDEN, C), RHIDDEN ** -0.5, 0.75, (), jnp.float32),
        "w_node": normal_values(splits[7], (C, C), C ** -0.5, 0.5, (), jnp.float32),
        "readout": normal_values(splits[8], (C,), C ** -0.5, 0.5, (), jnp.float32),
        "spectral_radius": jnp.clip(jnp.exp(jax.random.uniform(splits[9], (1,), jnp.float32, math.log(0.15), math.log(0.4))), 0.15, 0.4),
    }


SPACING = 2.2
CUTOFF = 5.0
NORM_SCALE = 0.22360679774997896
MASSES = (28.0855, 15.999, 22.99)
HIGHEST = lax.Precision.HIGHEST

def species_rows(species_ids, lookup_table):
    onehot = (species_ids[..., None] == jnp.arange(lookup_table.shape[0], dtype=jnp.int32)).astype(jnp.float32)
    return jnp.dot(onehot, lookup_table, precision=HIGHEST)

def radial_terms(distance, filled, w_radial1, w_radial2):

    def radial(radius_in):
        frequency = jnp.arange(1, w_radial1.shape[0] + 1).astype(jnp.float32) * (math.pi / CUTOFF)
        bessel = math.sqrt(2.0 / CUTOFF) * jnp.sin(radius_in[..., None] * frequency) / radius_in[..., None]
        scaled = radius_in / CUTOFF
        envelope = jnp.where(filled, (1.0 - scaled * scaled) ** 2, 0.0)
        hidden = jax.nn.silu(jnp.dot(bessel, w_radial1, precision=HIGHEST))
        return jnp.dot(hidden, w_radial2, precision=HIGHEST) * envelope[..., None]
    unit_tangent = jnp.ones_like(distance)

    def slope(radius_in):
        return jax.jvp(radial, (radius_in,), (unit_tangent,))
    (radial_value, first_order), (unused, second_order) = jax.jvp(slope, (distance,), (unit_tangent,))
    return (radial_value, first_order, second_order)

def edge_distance(positions, centres, neighbours, lattice, filled):
    edge_vec = lattice + jnp.moveaxis(positions[:, neighbours], 0, -1) - jnp.moveaxis(positions[:, centres], 0, -1)[:, None, :]
    return jnp.sqrt(jnp.where(filled, lax.optimization_barrier(jnp.sum(edge_vec * edge_vec, -1)), 1.0))

def plane_tables(positions, flat_species, centres, neighbours, slot_codes, embedding, w_radial1, w_radial2):
    step_x = slot_codes // 9 - 1
    step_y = slot_codes // 3 % 3 - 1
    step_z = slot_codes % 3 - 1
    lattice = jnp.stack([step_x, step_y, step_z], -1).astype(jnp.float32) * SPACING
    filled = slot_codes != 13
    distance = edge_distance(positions, centres, neighbours, lattice, filled)
    radial_value, first_order, second_order = radial_terms(distance, filled, w_radial1, w_radial2)
    neighbour_rows = species_rows(flat_species[neighbours], embedding) * NORM_SCALE
    message_base = lax.optimization_barrier(jnp.sum(radial_value * neighbour_rows, 1))
    centre_rows = species_rows(flat_species[centres], embedding)
    return (centres, neighbours, lattice, filled, distance, message_base, first_order * neighbour_rows, second_order * neighbour_rows, centre_rows)

def taylor_energy(positions, tables, w_node, readout):
    centres, neighbours, lattice, filled, base_distance, message_base, first_order, second_order, centre_rows = tables
    change = edge_distance(positions, centres, neighbours, lattice, filled) - base_distance
    message = message_base + jnp.einsum('cn,cnk->ck', change, first_order, precision=HIGHEST)
    message = message + 0.5 * jnp.einsum('cn,cnk->ck', change * change, second_order, precision=HIGHEST)
    node_feat = jax.nn.silu(jnp.dot(message, w_node, precision=HIGHEST) + centre_rows)
    return jnp.sum(jnp.dot(node_feat, readout, precision=HIGHEST))

def reference(displacements, species, neighbor_index, probes, embedding, w_radial1, w_radial2, w_node, readout, spectral_radius):
    atom_total = NX * NY * NZ
    plane_size = NY * NZ
    index_shape = neighbor_index.shape
    grid_x = lax.broadcasted_iota(jnp.int32, index_shape, 1)
    grid_y = lax.broadcasted_iota(jnp.int32, index_shape, 2)
    grid_z = lax.broadcasted_iota(jnp.int32, index_shape, 3)
    depth_y = CY + 2
    depth_z = CZ + 2
    step_x = neighbor_index // (depth_y * depth_z) - grid_x % CX - 1
    step_y = neighbor_index // depth_z % depth_y - grid_y % CY - 1
    step_z = neighbor_index % depth_z - grid_z % CZ - 1
    slot_codes = (step_x + 1) * 9 + (step_y + 1) * 3 + step_z + 1
    target = (grid_x + step_x) % NX * plane_size + (grid_y + step_y) % NY * NZ + (grid_z + step_z) % NZ
    neighbours_all = jnp.transpose(target.reshape(NEIGH, NX, plane_size), (1, 2, 0)).astype(jnp.int32)
    codes_all = jnp.transpose(slot_codes.reshape(NEIGH, NX, plane_size), (1, 2, 0)).astype(jnp.int32)
    positions = displacements.reshape(3, atom_total)
    flat_species = species.reshape(atom_total)
    masses = species_rows(species, jnp.array(MASSES, dtype=jnp.float32)[:, None])[..., 0]
    inv_root = 1.0 / jnp.sqrt(masses)

    def hessian(vectors):

        def add_plane(running, plane_item):
            plane_index, neighbours, plane_codes = plane_item
            centres = plane_index * plane_size + jnp.arange(plane_size, dtype=jnp.int32)
            tables = plane_tables(positions, flat_species, centres, neighbours, plane_codes, embedding, w_radial1, w_radial2)
            force_field = jax.grad(lambda moved: taylor_energy(moved, tables, w_node, readout))
            result = jax.vmap(lambda vector: jax.jvp(force_field, (positions,), (vector,))[1])(vectors)
            return (running + result, None)
        summed, unused = lax.scan(add_plane, jnp.zeros(vectors.shape, jnp.float32), (jnp.arange(NX, dtype=jnp.int32), neighbours_all, codes_all))
        return summed

    def operate(vectors):
        scaled = (vectors * inv_root).reshape(PROBES, 3, atom_total)
        product = hessian(scaled).reshape(vectors.shape)
        return product * inv_root / spectral_radius[0]
    previous = probes
    current = operate(probes)
    partials = [lax.optimization_barrier(jnp.sum(probes * probes, axis=(1, 2, 3, 4))), lax.optimization_barrier(jnp.sum(probes * current, axis=(1, 2, 3, 4)))]
    for iteration in range(2, STEPS + 1):
        following = 2.0 * operate(current) - previous
        previous, current = (current, following)
        partials.append(lax.optimization_barrier(jnp.sum(probes * current, axis=(1, 2, 3, 4))))
    return (jnp.stack([previous, current]), jnp.stack(partials))
```

```python
import functools
import math

import jax
import jax.numpy as jnp
from jax import lax
from jax.experimental import pallas as pl
from jax.experimental.pallas import tpu as pltpu
from jax.sharding import PartitionSpec as P

SPACING = 2.2
CUTOFF = 5.0
NORM_SCALE = 0.22360679774997896
MASSES = (28.0855, 15.999, 22.99)
HIGHEST = lax.Precision.HIGHEST
MESH = pl.DeviceIdType.MESH
F32 = jnp.float32
BF16 = jnp.bfloat16

CODES = tuple(c for c in range(27) if c != 13)
ORDER = {c: n for n, c in enumerate(CODES)}
NC = len(CODES)
AXES = ("gx", "gy", "gz")
LANES = 128
HID = 64
PROBES = 8


def step_of(code):
    return code // 9 - 1, code // 3 % 3 - 1, code % 3 - 1


def roll(value, by):
    return pltpu.roll(value, by % LANES, 1)


def high_low(value):
    high = value.astype(BF16).astype(F32)
    return high, value - high


def by_species(species, values):
    return jnp.where(species < 0.5, values[0], jnp.where(species < 1.5, values[1], values[2]))


def sin_cos(angle):
    off = angle - math.pi / 2
    square = off * off
    odd = jnp.full_like(off, -1.0 / math.factorial(15))
    for power in (13, 11, 9, 7, 5, 3, 1):
        odd = odd * square + (-1.0) ** (power // 2) / math.factorial(power)
    even = jnp.full_like(off, 1.0 / math.factorial(16))
    for power in (14, 12, 10, 8, 6, 4, 2, 0):
        even = even * square + (-1.0) ** (power // 2) / math.factorial(power)
    return even, -odd * off


class Lanes:
    def __init__(self):
        lane = lax.broadcasted_iota(jnp.int32, (8, LANES), 1)
        self.lane = lane
        self.x = lane >= 64
        self.y = (lane & 32) != 0
        self.z = lane & 31
        self.z_low = self.z == 0
        self.z_high = self.z == 31

    def swap(self, axis, value):
        if axis == 0:
            return roll(value, 64)
        return jnp.where(self.y, roll(value, 32), roll(value, -32))

    def upper(self, axis):
        return self.x if axis == 0 else self.y


def gather(lanes, ext):
    along_x = {}
    for gy in (0, 1):
        for gz in (0, 1):
            own, ghost = ext[0][gy][gz], ext[1][gy][gz]
            along_x[0, gy, gz] = own
            along_x[1, gy, gz] = lanes.swap(0, jnp.where(lanes.x, own, ghost))
            along_x[-1, gy, gz] = lanes.swap(0, jnp.where(lanes.x, ghost, own))
    out = {}
    for sx in (-1, 0, 1):
        along_y = {}
        for gz in (0, 1):
            own, ghost = along_x[sx, 0, gz], along_x[sx, 1, gz]
            along_y[0, gz] = own
            along_y[1, gz] = lanes.swap(1, jnp.where(lanes.y, own, ghost))
            along_y[-1, gz] = lanes.swap(1, jnp.where(lanes.y, ghost, own))
        for sy in (-1, 0, 1):
            own, ghost = along_y[sy, 0], along_y[sy, 1]
            base = (sx + 1) * 9 + (sy + 1) * 3 + 1
            out[base] = own
            out[base + 1] = jnp.where(lanes.z_high, roll(ghost, 31), roll(own, -1))
            out[base - 1] = jnp.where(lanes.z_low, roll(ghost, -31), roll(own, 1))
    return out


def scatter(lanes, edges):
    along_z = {}
    for sx in (-1, 0, 1):
        for sy in (-1, 0, 1):
            base = (sx + 1) * 9 + (sy + 1) * 3 + 1
            up, down = edges(base + 1), edges(base - 1)
            own = edges(base)
            own = own + jnp.where(lanes.z_low, 0.0, roll(up, 1))
            own = own + jnp.where(lanes.z_high, 0.0, roll(down, -1))
            ghost = jnp.where(
                lanes.z_low, roll(up, -31), jnp.where(lanes.z_high, roll(down, 31), 0.0)
            )
            along_z[sx, sy, 0], along_z[sx, sy, 1] = own, ghost
    along_y = {}
    for sx in (-1, 0, 1):
        for gz in (0, 1):
            up, down = along_z[sx, 1, gz], along_z[sx, -1, gz]
            along_y[sx, 0, gz] = along_z[sx, 0, gz] + lanes.swap(1, jnp.where(lanes.y, down, up))
            along_y[sx, 1, gz] = lanes.swap(1, jnp.where(lanes.y, up, down))
    ext = [[[None, None], [None, None]], [[None, None], [None, None]]]
    for gy in (0, 1):
        for gz in (0, 1):
            up, down = along_y[1, gy, gz], along_y[-1, gy, gz]
            ext[0][gy][gz] = along_y[0, gy, gz] + lanes.swap(0, jnp.where(lanes.x, down, up))
            ext[1][gy][gz] = lanes.swap(0, jnp.where(lanes.x, up, down))
    return ext


def kernel(
    sizes,
    radius_ref,
    pack_ref,
    emb_ref,
    w1_ref,
    w2_ref,
    wn_ref,
    readout_ref,
    cheb_ref,
    moments_ref,
    halo_send,
    halo_recv,
    fold_send,
    fold_recv,
    sum_send,
    sum_recv,
    halo_sems,
    fold_sems,
    sum_sems,
    geo_ref,
    trig_ref,
    rows_ref,
    acc_ref,
    prod_ref,
    second_ref,
    node_ref,
    matrix_ref,
    dv_ref,
    dr_ref,
    edge_ref,
    small_ref,
):
    place = [lax.axis_index(axis) for axis in AXES]

    def partner(axis, by):
        return lax.rem(place[axis] + (by + sizes[axis]), sizes[axis])

    barrier = pltpu.get_barrier_semaphore()
    partners = [(axis, by) for axis in range(3) for by in range(1, sizes[axis])]
    for axis, by in partners:
        pl.semaphore_signal(
            barrier, inc=1, device_id={AXES[axis]: partner(axis, by)}, device_id_type=MESH
        )

    lanes = Lanes()
    species = pack_ref[3:4, :]
    inv_root = by_species(species, [1.0 / math.sqrt(m) for m in MASSES])
    root = by_species(species, [math.sqrt(m) for m in MASSES])
    probes = [pack_ref[pl.ds(8 + j, PROBES, stride=3), :] for j in range(3)]
    start = [p * inv_root for p in probes]
    own_halo = start + [pack_ref[0:8, :]]

    pl.semaphore_wait(barrier, len(partners))

    def copy(src, dst, sems, number, axis, by):
        return pltpu.make_async_remote_copy(
            src_ref=src,
            dst_ref=dst,
            send_sem=sems.at[0, number],
            recv_sem=sems.at[1, number],
            device_id={AXES[axis]: partner(axis, by)},
            device_id_type=MESH,
        )

    def merge(axis, low_value, high_value):
        if axis < 2:
            return jnp.where(lanes.upper(axis), high_value, low_value)
        return jnp.where(lanes.z_low, low_value, jnp.where(lanes.z_high, high_value, 0.0))

    def halo_start(axis, held):
        for n, array in enumerate(held):
            for v in range(4):
                halo_send[axis, pl.ds(8 * (4 * n + v), 8), :] = array[v]
        rows = pl.ds(0, 32 * len(held))
        copies = [
            copy(
                halo_send.at[axis, rows],
                halo_recv.at[axis, d, rows],
                halo_sems,
                2 * axis + d,
                axis,
                1 if d == 0 else -1,
            )
            for d in (0, 1)
        ]
        for c in copies:
            c.start()
        return copies

    def halo_finish(axis, held, copies):
        for c in copies:
            c.wait()
        ghosts = []
        for n in range(len(held)):
            ghost = []
            for v in range(4):
                rows = pl.ds(8 * (4 * n + v), 8)
                ghost.append(merge(axis, halo_recv[axis, 1, rows, :], halo_recv[axis, 0, rows, :]))
            ghosts.append(ghost)
        return held + ghosts

    held = [own_halo]
    copies = halo_start(0, held)

    for s in range(3):
        acc_ref[pl.ds(64 * s, 64), :] = w2_ref[...] * emb_ref[s : s + 1, :]
    to_node = jnp.dot(
        acc_ref[...], wn_ref[...], precision=HIGHEST, preferred_element_type=F32
    ) * NORM_SCALE
    flipped = [jnp.transpose(to_node[64 * s : 64 * s + 64, :]) for s in range(3)]
    flip = [high_low(f) for f in flipped]
    left_node = jnp.concatenate(
        [jnp.concatenate([hi, hi, lo], axis=1) for hi, lo in flip], axis=0
    ).astype(BF16)
    first_high, first_low = high_low(w1_ref[...] * math.sqrt(2.0 / CUTOFF))
    left_radial = jnp.transpose(
        jnp.concatenate([first_high, first_high, first_low, jnp.zeros_like(first_high)], axis=0)
    ).astype(BF16)
    small_ref[0:8, :] = jnp.zeros((8, LANES), F32)
    small_ref[0:3, :] = emb_ref[...]
    small_ref[3:4, :] = readout_ref[...]
    columns = jnp.transpose(small_ref[0:8, :])
    readout = columns[:, 3:4]

    row_lane = lax.broadcasted_iota(jnp.int32, (32, LANES), 1)
    home = (
        ((row_lane >> 6) + 1) * (4 * 34) + (((row_lane >> 5) & 1) + 1) * 34 + (row_lane & 31) + 1
    )
    off = pack_ref[32:64, :].astype(jnp.int32) - home

    def unit(value, bound):
        return jnp.where(value > bound, 1, 0) - jnp.where(value < -bound, 1, 0)

    off_x = unit(off, 68)
    rest = off - 136 * off_x
    off_y = unit(rest, 17)
    off_z = rest - 34 * off_y
    code = (off_x + 1) * 9 + (off_y + 1) * 3 + off_z + 1
    bits = jnp.where(off == 0, 0, jnp.left_shift(jnp.ones_like(code), code))
    bits = jnp.sum(bits, axis=0, keepdims=True)

    for axis in range(3):
        held = halo_finish(axis, held, copies)
        if axis < 2:
            copies = halo_start(axis + 1, held)

    def ext_of(v):
        return [[[held[gx + 2 * gy + 4 * gz][v] for gz in (0, 1)] for gy in (0, 1)] for gx in (0, 1)]

    geometry = ext_of(3)
    y_old = [ext_of(j) for j in range(3)]
    scale = 1.0 / radius_ref[0]
    weight_sq = [
        [
            [by_species(geometry[gx][gy][gz][3:4, :], [1.0 / m for m in MASSES]) * scale for gz in (0, 1)]
            for gy in (0, 1)
        ]
        for gx in (0, 1)
    ]

    seen = gather(lanes, geometry)
    for n, c in enumerate(CODES):
        geo_ref[pl.ds(8 * n, 8), :] = seen[c]
        rows_ref[9, pl.ds(n, 1), :] = (jnp.right_shift(bits, c) & 1).astype(F32)
    code_row = lax.broadcasted_iota(jnp.int32, (NC, LANES), 0)
    code_row = code_row + jnp.where(code_row >= 13, 1, 0)
    off_z = code_row % 3
    off_y = (code_row // 3) % 3
    off_x = code_row // 9
    vectors = []
    for j, steps in enumerate((off_x, off_y, off_z)):
        vectors.append(
            (steps - 1).astype(F32) * SPACING
            + geo_ref[pl.ds(j, NC, stride=8), :]
            - pack_ref[j : j + 1, :]
        )
    filled = rows_ref[9, 0:NC, :]
    present = filled > 0.5
    square = vectors[0] * vectors[0] + vectors[1] * vectors[1] + vectors[2] * vectors[2]
    distance = jnp.sqrt(jnp.where(present, square, 1.0))
    inverse = 1.0 / distance
    part = distance * (1.0 / CUTOFF)
    part_sq = part * part
    for j in range(3):
        rows_ref[j, 0:NC, :] = vectors[j] * inverse
    rows_ref[3, 0:NC, :] = inverse
    rows_ref[4, 0:NC, :] = filled * (1.0 - part_sq) * (1.0 - part_sq)
    rows_ref[5, 0:NC, :] = filled * (-4.0 / CUTOFF) * part * (1.0 - part_sq)
    rows_ref[6, 0:NC, :] = filled * (-4.0 / CUTOFF**2) * (1.0 - 3.0 * part_sq)
    rows_ref[7, 0:NC, :] = geo_ref[pl.ds(3, NC, stride=8), :]
    sin_1, cos_1 = sin_cos(distance * (math.pi / CUTOFF))
    sin_k, cos_k = sin_1, cos_1
    sin_b, cos_b = jnp.zeros_like(sin_1), jnp.ones_like(cos_1)
    for k in range(8):
        omega = (k + 1) * math.pi / CUTOFF
        trig_ref[pl.ds(k, NC, stride=24), :] = sin_k
        trig_ref[pl.ds(8 + k, NC, stride=24), :] = cos_k * omega
        trig_ref[pl.ds(16 + k, NC, stride=24), :] = sin_k * (-omega * omega)
        sin_k, sin_b = 2.0 * cos_1 * sin_k - sin_b, sin_k
        cos_k, cos_b = 2.0 * cos_1 * cos_k - cos_b, cos_k

    acc_ref[...] = jnp.zeros_like(acc_ref)

    def radial(pair, carry):
        blocks = []
        for i in (0, 1):
            for g in range(3):
                hi, lo = high_low(trig_ref[pl.ds((2 * pair + i) * 24 + 8 * g, 8), :])
                blocks.append(jnp.concatenate([hi, lo, hi, jnp.zeros_like(hi)], axis=0))
        right = jnp.concatenate(blocks, axis=1).astype(BF16)
        waves = jnp.dot(left_radial, right, preferred_element_type=F32)
        rights = []
        for i in (0, 1):
            n = 2 * pair + i
            wave = [waves[:, 128 * (3 * i + g) : 128 * (3 * i + g + 1)] for g in range(3)]
            inv = rows_ref[3, pl.ds(n, 1), :]
            env = [rows_ref[4 + g, pl.ds(n, 1), :] for g in range(3)]
            kind = rows_ref[7, pl.ds(n, 1), :]
            x_0 = wave[0] * inv
            x_1 = (wave[1] - x_0) * inv
            x_2 = (wave[2] - 2.0 * x_1) * inv
            gate = 1.0 / (1.0 + jnp.exp(-x_0))
            shut = 1.0 - gate
            value = x_0 * gate
            slope = gate + value * shut
            bend = shut * (2.0 * gate + value * (1.0 - 2.0 * gate))
            r_1 = slope * x_1
            r_2 = bend * x_1 * x_1 + slope * x_2
            h_0 = value * env[0]
            h_1 = r_1 * env[0] + value * env[1]
            h_2 = r_2 * env[0] + 2.0 * r_1 * env[1] + value * env[2]
            second_ref[n] = h_2
            for s in range(3):
                one = jnp.where(jnp.abs(kind - s) < 0.5, 1.0, 0.0)
                acc_ref[pl.ds(64 * s, 64), :] += h_0 * one
            hi, lo = high_low(h_1)
            rights.append(jnp.concatenate([hi, lo, hi], axis=0).astype(BF16))
        product = jnp.dot(
            left_node, jnp.concatenate(rights, axis=1), preferred_element_type=F32
        )
        for i in (0, 1):
            n = 2 * pair + i
            kind = rows_ref[7, pl.ds(n, 1), :]
            cols = slice(128 * i, 128 * i + 128)
            prod_ref[n] = by_species(
                kind, [product[128 * s : 128 * s + 128, cols] for s in range(3)]
            )
        return carry

    lax.fori_loop(0, NC // 2, radial, 0)

    home_kind = jnp.where(
        lax.broadcasted_iota(jnp.int32, (8, LANES), 0).astype(F32) == species, 1.0, 0.0
    )
    home_kind = jnp.where(lax.broadcasted_iota(jnp.int32, (8, LANES), 0) < 3, home_kind, 0.0)
    node = jnp.dot(columns, home_kind, precision=HIGHEST, preferred_element_type=F32)
    node = node + jnp.dot(
        jnp.concatenate(flipped, axis=1), acc_ref[...], precision=HIGHEST, preferred_element_type=F32
    )
    gate = 1.0 / (1.0 + jnp.exp(-node))
    shut = 1.0 - gate
    value = node * gate
    node_slope = readout * (gate + value * shut)
    node_ref[0] = node_slope
    node_ref[1] = readout * (shut * (2.0 * gate + value * (1.0 - 2.0 * gate)))
    acc_ref[...] = jnp.dot(to_node, node_slope, precision=HIGHEST, preferred_element_type=F32)

    def edge_matrix(n, carry):
        mine = prod_ref[n]
        kind = rows_ref[7, pl.ds(n, 1), :]
        pull = jnp.sum(mine * node_ref[0], axis=0, keepdims=True) * rows_ref[3, pl.ds(n, 1), :]
        back = by_species(kind, [acc_ref[64 * s : 64 * s + 64, :] for s in range(3)])
        curve = jnp.sum(back * second_ref[n], axis=0, keepdims=True)
        rows_ref[8, pl.ds(n, 1), :] = pull
        bent = mine * node_ref[1]
        for m in range(NC):
            both = jnp.sum(bent * prod_ref[m], axis=0, keepdims=True)
            matrix_ref[n * NC + m] = jnp.broadcast_to(both, (8, LANES))
        matrix_ref[n * NC + n] = matrix_ref[n * NC + n] + (curve - pull)
        return carry

    lax.fori_loop(0, NC, edge_matrix, 0)

    def local_product(y):
        for j in range(3):
            views = gather(lanes, y[j])
            for n, c in enumerate(CODES):
                dv_ref[3 * n + j] = views[c] - views[13]

        def along(n, carry):
            total = jnp.zeros((8, LANES), F32)
            for j in range(3):
                total = total + rows_ref[j, pl.ds(n, 1), :] * dv_ref[3 * n + j]
            dr_ref[n] = total
            return carry

        lax.fori_loop(0, NC, along, 0, unroll=True)

        def force(n, carry):
            total = matrix_ref[n * NC] * dr_ref[0]
            for m in range(1, NC):
                total = total + matrix_ref[n * NC + m] * dr_ref[m]
            pull = rows_ref[8, pl.ds(n, 1), :]
            out = []
            for j in range(3):
                edge = rows_ref[j, pl.ds(n, 1), :] * total + pull * dv_ref[3 * n + j]
                edge_ref[3 * n + j] = edge
                out.append(carry[j] - edge)
            return tuple(out)

        zero = jnp.zeros((8, LANES), F32)
        centre = lax.fori_loop(0, NC, force, (zero, zero, zero))
        return [
            scatter(lanes, lambda c, j=j: centre[j] if c == 13 else edge_ref[3 * ORDER[c] + j])
            for j in range(3)
        ]

    def exchange(number, terms, own_only, beside):
        held = {
            (gx, gy, gz): [terms[j][gx][gy][gz] for j in range(3)]
            for gx in (0, 1)
            for gy in (0, 1)
            for gz in (0, 1)
        }
        for axis in range(3):
            owns = sorted(k for k in held if k[axis] == 0)
            count = 3 * len(owns)
            for n, key in enumerate(owns):
                other = key[:axis] + (1,) + key[axis + 1 :]
                for j in range(3):
                    own, ghost = held[key][j], held[other][j]
                    rows = pl.ds(8 * (3 * n + j), 8)
                    if axis < 2:
                        low = jnp.logical_not(lanes.upper(axis))
                        high = lanes.upper(axis)
                    else:
                        low, high = lanes.z_low, lanes.z_high
                    fold_send[number, axis, 0, rows, :] = jnp.where(low, ghost, own)
                    fold_send[number, axis, 1, rows, :] = jnp.where(high, ghost, own)
            rows = pl.ds(0, 8 * count)
            copies = [
                copy(
                    fold_send.at[number, axis, d, rows],
                    fold_recv.at[number, axis, d, rows],
                    fold_sems.at[number],
                    2 * axis + d,
                    axis,
                    1 if d == 0 else -1,
                )
                for d in (0, 1)
            ]
            for c in copies:
                c.start()
            beside(axis)
            for c in copies:
                c.wait()
            after = {}
            for n, key in enumerate(owns):
                other = key[:axis] + (1,) + key[axis + 1 :]
                own_sum, ghost_sum = [], []
                for j in range(3):
                    rows = pl.ds(8 * (3 * n + j), 8)
                    below = fold_recv[number, axis, 0, rows, :]
                    above = fold_recv[number, axis, 1, rows, :]
                    own_sum.append(held[key][j] + merge(axis, below, above))
                    ghost_sum.append(held[other][j] + merge(axis, above, below))
                after[key] = own_sum
                if not own_only:
                    after[other] = ghost_sum
            held = after
        return held

    def advance(product, factor, before):
        return [
            [
                [
                    [
                        product[gx, gy, gz][j] * (weight_sq[gx][gy][gz] * factor)
                        - (0.0 if before is None else before[j][gx][gy][gz])
                        for gz in (0, 1)
                    ]
                    for gy in (0, 1)
                ]
                for gx in (0, 1)
            ]
            for j in range(3)
        ]

    def nothing(axis):
        return None

    product = exchange(0, local_product(y_old), False, nothing)
    y_1 = advance(product, 1.0, None)
    product = exchange(1, local_product(y_1), False, nothing)
    y_2 = advance(product, 2.0, y_old)
    t_1 = [y_1[j][0][0][0] * root for j in range(3)]
    t_2 = [y_2[j][0][0][0] * root for j in range(3)]
    for j in range(3):
        cheb_ref[0, pl.ds(j, PROBES, stride=3), :] = t_2[j]

    terms = [
        sum(probes[j] * probes[j] for j in range(3)),
        sum(probes[j] * t_1[j] for j in range(3)),
        sum(probes[j] * t_2[j] for j in range(3)),
        sum((2.0 * t_2[j] - probes[j]) * t_1[j] for j in range(3)),
    ]
    packed = jnp.zeros((8, LANES), F32)
    for k in range(4):
        packed = jnp.where(lanes.lane == k, jnp.sum(terms[k], axis=1, keepdims=True), packed)
    moments_ref[...] = packed

    def sum_start(axis):
        sum_send[axis] = moments_ref[...]
        copies = []
        for by in range(1, sizes[axis]):
            c = copy(
                sum_send.at[axis],
                sum_recv.at[axis, by],
                sum_sems.at[axis],
                by,
                axis,
                by,
            )
            c.start()
            copies.append(c)
        return copies

    def sum_finish(axis, copies):
        for c in copies:
            c.wait()
        sum_recv[axis, 0] = sum_send[axis]
        total = jnp.zeros((8, LANES), F32)
        for index in range(sizes[axis]):
            slot = lax.rem(place[axis] + (sizes[axis] - index), sizes[axis])
            total = total + sum_recv[axis, slot]
        moments_ref[...] = total

    terms_3 = local_product(y_2)
    flight = {}

    def beside(axis):
        if axis > 0:
            sum_finish(axis - 1, flight.pop(axis - 1))
        flight[axis] = sum_start(axis)

    product = exchange(2, terms_3, True, beside)
    own_weight = weight_sq[0][0][0] * 2.0 * root
    for j in range(3):
        cheb_ref[1, pl.ds(j, PROBES, stride=3), :] = product[0, 0, 0][j] * own_weight - t_1[j]
    sum_finish(2, flight.pop(2))


def on_device(
    sizes,
    displacements,
    species,
    neighbor_index,
    probes,
    embedding,
    w_radial1,
    w_radial2,
    w_node,
    readout,
    spectral_radius,
):
    site = species.shape
    pack = jnp.concatenate(
        [
            displacements,
            species.astype(F32)[None],
            jnp.zeros((4,) + site, F32),
            probes.reshape((3 * PROBES,) + site),
            neighbor_index.astype(F32),
        ],
        axis=0,
    ).reshape(64, LANES)
    vmem = pl.BlockSpec(memory_space=pltpu.VMEM)
    most = max(sizes)
    cheb, moments = pl.pallas_call(
        functools.partial(kernel, sizes),
        out_shape=(
            jax.ShapeDtypeStruct((2, 3 * PROBES, LANES), F32),
            jax.ShapeDtypeStruct((8, LANES), F32),
        ),
        in_specs=[pl.BlockSpec(memory_space=pltpu.SMEM)] + [vmem] * 6,
        out_specs=(vmem, vmem),
        scratch_shapes=[
            pltpu.VMEM((3, 128, LANES), F32),
            pltpu.VMEM((3, 2, 128, LANES), F32),
            pltpu.VMEM((3, 3, 2, 96, LANES), F32),
            pltpu.VMEM((3, 3, 2, 96, LANES), F32),
            pltpu.VMEM((3, 8, LANES), F32),
            pltpu.VMEM((3, most, 8, LANES), F32),
            pltpu.SemaphoreType.DMA((2, 6)),
            pltpu.SemaphoreType.DMA((3, 2, 6)),
            pltpu.SemaphoreType.DMA((3, 2, most)),
            pltpu.VMEM((8 * NC, LANES), F32),
            pltpu.VMEM((24 * NC, LANES), F32),
            pltpu.VMEM((10, 32, LANES), F32),
            pltpu.VMEM((3 * HID, LANES), F32),
            pltpu.VMEM((NC, 128, LANES), F32),
            pltpu.VMEM((NC, HID, LANES), F32),
            pltpu.VMEM((2, 128, LANES), F32),
            pltpu.VMEM((NC * NC, 8, LANES), F32),
            pltpu.VMEM((3 * NC, 8, LANES), F32),
            pltpu.VMEM((NC, 8, LANES), F32),
            pltpu.VMEM((3 * NC, 8, LANES), F32),
            pltpu.VMEM((8, LANES), F32),
        ],
        compiler_params=pltpu.CompilerParams(
            collective_id=0, has_side_effects=True, vmem_limit_bytes=40 * 2**20
        ),
        name="chebyshev",
    )(
        spectral_radius,
        pack,
        embedding,
        w_radial1,
        w_radial2,
        w_node,
        readout.reshape(1, -1),
    )
    return cheb.reshape((2,) + probes.shape), moments[:, :4].T


def solution(mesh):
    placed = (
        P(None, "gx", "gy", "gz"),
        P("gx", "gy", "gz"),
        P(None, "gx", "gy", "gz"),
        P(None, None, "gx", "gy", "gz"),
        P(),
        P(),
        P(),
        P(),
        P(),
        P(),
    )
    return jax.shard_map(
        functools.partial(on_device, tuple(mesh.shape[axis] for axis in AXES)),
        mesh=mesh,
        in_specs=placed,
        out_specs=(P(None, None, None, "gx", "gy", "gz"), P()),
        check_vma=False,
    )
```

```python
import functools
import math

import jax
import jax.numpy as jnp
from jax import lax
from jax.experimental import pallas as pl
from jax.experimental.pallas import tpu as pltpu
from jax.sharding import PartitionSpec as P

SPACING = 2.2
CUTOFF = 5.0
NORM_SCALE = 0.22360679774997896
MASSES = (28.0855, 15.999, 22.99)
HIGHEST = lax.Precision.HIGHEST
MESH = pl.DeviceIdType.MESH
F32 = jnp.float32
BF16 = jnp.bfloat16

CODES = tuple(sorted((c for c in range(27) if c != 13), key=lambda c: (c % 3 != 1, c)))
ORDER = {c: n for n, c in enumerate(CODES)}
NC = len(CODES)
FLAT = 8
BLOCKS = ((0, 7), (7, 14), (14, 20), (20, 26))
AXES = ("gx", "gy", "gz")
LANES = 128
HID = 64
PROBES = 8


def roll(value, by):
    return pltpu.roll(value, by % LANES, 1)


def high_low(value):
    high = value.astype(BF16).astype(F32)
    return high, value - high


def by_species(species, values):
    return jnp.where(species < 0.5, values[0], jnp.where(species < 1.5, values[1], values[2]))


def sin_cos(angle):
    off = angle - math.pi / 2
    square = off * off
    odd = jnp.full_like(off, -1.0 / math.factorial(15))
    for power in (13, 11, 9, 7, 5, 3, 1):
        odd = odd * square + (-1.0) ** (power // 2) / math.factorial(power)
    even = jnp.full_like(off, 1.0 / math.factorial(16))
    for power in (14, 12, 10, 8, 6, 4, 2, 0):
        even = even * square + (-1.0) ** (power // 2) / math.factorial(power)
    return even, -odd * off


class Lanes:
    def __init__(self):
        lane = lax.broadcasted_iota(jnp.int32, (8, LANES), 1)
        self.lane = lane
        self.upper = (lane >= 64, (lane & 32) != 0)
        self.z = lane & 31
        self.low_z = self.z < 16
        self.first = [self.z == j for j in range(3)]
        self.last = [self.z == 31 - j for j in range(3)]

    def swap(self, axis, value):
        if axis == 0:
            return roll(value, 64)
        return jnp.where(self.upper[1], roll(value, 32), roll(value, -32))

    def merge(self, axis, low_value, high_value):
        if axis < 2:
            return jnp.where(self.upper[axis], high_value, low_value)
        return jnp.where(self.low_z, low_value, high_value)

    def ends(self, low_values, high_values):
        out = jnp.zeros((8, LANES), F32)
        for j, (low, high) in enumerate(zip(low_values, high_values)):
            out = jnp.where(self.first[j], low, jnp.where(self.last[j], high, out))
        return out

    def pack(self, values):
        return self.ends(
            [roll(v, j) if j else v for j, v in enumerate(values)],
            [roll(v, -j) if j else v for j, v in enumerate(values)],
        )

    def unpack(self, packed, count):
        out = []
        for j in range(count):
            low, high = (roll(packed, -j), roll(packed, j)) if j else (packed, packed)
            out.append(jnp.where(self.first[0], low, jnp.where(self.last[0], high, 0.0)))
        return out


SITES = tuple((gx, gy) for gx in (0, 1) for gy in (0, 1))


def gather(lanes, ext, flat_only=False):
    count = len(ext[0, 0]) - 1
    along_x = {}
    for gy in (0, 1):
        own, ghost = ext[0, gy], ext[1, gy]
        along_x[0, gy] = own
        along_x[1, gy] = [lanes.swap(0, lanes.merge(0, g, o)) for o, g in zip(own, ghost)]
        along_x[-1, gy] = [lanes.swap(0, lanes.merge(0, o, g)) for o, g in zip(own, ghost)]
    out = {}
    for sx in (-1, 0, 1):
        own, ghost = along_x[sx, 0], along_x[sx, 1]
        along_y = {
            0: own,
            1: [lanes.swap(1, lanes.merge(1, g, o)) for o, g in zip(own, ghost)],
            -1: [lanes.swap(1, lanes.merge(1, o, g)) for o, g in zip(own, ghost)],
        }
        for sy in (-1, 0, 1):
            values, packed = along_y[sy][:count], along_y[sy][count]
            base = (sx + 1) * 9 + (sy + 1) * 3 + 1
            out[base] = values
            if flat_only:
                continue
            out[base + 1] = [
                jnp.where(lanes.last[0], roll(packed, 31 - j), roll(v, -1))
                for j, v in enumerate(values)
            ]
            out[base - 1] = [
                jnp.where(lanes.first[0], roll(packed, j - 31), roll(v, 1))
                for j, v in enumerate(values)
            ]
    return out


def scatter(lanes, edges):
    along_z = {}
    for sx in (-1, 0, 1):
        for sy in (-1, 0, 1):
            base = (sx + 1) * 9 + (sy + 1) * 3 + 1
            values, lows, highs = [], [], []
            for j in range(3):
                up, down = edges(base + 1, j), edges(base - 1, j)
                own = edges(base, j)
                own = own + jnp.where(lanes.first[0], 0.0, roll(up, 1))
                values.append(own + jnp.where(lanes.last[0], 0.0, roll(down, -1)))
                lows.append(roll(up, j - 31))
                highs.append(roll(down, 31 - j))
            along_z[sx, sy] = values + [lanes.ends(lows, highs)]
    along_y = {}
    for sx in (-1, 0, 1):
        items = list(zip(along_z[sx, -1], along_z[sx, 0], along_z[sx, 1]))
        along_y[sx, 0] = [m + lanes.swap(1, lanes.merge(1, up, down)) for down, m, up in items]
        along_y[sx, 1] = [lanes.swap(1, lanes.merge(1, down, up)) for down, m, up in items]
    ext = {}
    for gy in (0, 1):
        items = list(zip(along_y[-1, gy], along_y[0, gy], along_y[1, gy]))
        ext[0, gy] = [m + lanes.swap(0, lanes.merge(0, up, down)) for down, m, up in items]
        ext[1, gy] = [lanes.swap(0, lanes.merge(0, down, up)) for down, m, up in items]
    return ext


def kernel(
    sizes,
    radius_ref,
    *refs,
):
    sources, refs = refs[:9], refs[9:]
    (
        cheb_ref,
        result_ref,
        moments_ref,
        geo_send,
        geo_recv,
        halo_send,
        halo_recv,
        fold_send,
        fold_recv,
        sum_send,
        sum_recv,
        geo_sems,
        halo_sems,
        fold_sems,
        sum_sems,
        geo_ref,
        trig_ref,
        rows_ref,
        acc_ref,
        prod_ref,
        second_ref,
        node_ref,
        matrix_ref,
        dv_ref,
        dr_ref,
        edge_ref,
        small_ref,
        pack_ref,
    ) = refs[: -10]
    fetched, fetch_sems = refs[-10:-1], refs[-1]
    disp_ref, species_ref, index_ref, probes_ref, emb_ref, w1_ref, w2_ref, wn_ref, readout_ref = fetched
    fetches = [
        pltpu.make_async_copy(src, dst, fetch_sems.at[n])
        for n, (src, dst) in enumerate(zip(sources, fetched))
    ]
    for n in (0, 1, 3, 4, 5, 6, 7, 8, 2):
        fetches[n].start()

    place = [lax.axis_index(axis) for axis in AXES]

    def partner(axis, by):
        return lax.rem(place[axis] + (by + sizes[axis]), sizes[axis])

    barrier = pltpu.get_barrier_semaphore()
    partners = [(axis, by) for axis in range(3) for by in range(1, sizes[axis])]
    for axis, by in partners:
        pl.semaphore_signal(
            barrier, inc=1, device_id={AXES[axis]: partner(axis, by)}, device_id_type=MESH
        )

    def flat(ref, first, count, stride):
        return jnp.concatenate(
            [ref[pl.ds(first + q, count, stride=stride), :] for q in range(4)], axis=1
        )

    lanes = Lanes()
    pack_ref[0:8, :] = jnp.zeros((8, LANES), F32)
    for n in (0, 1):
        fetches[n].wait()
    pack_ref[0:3, :] = jnp.concatenate([disp_ref[:, q, :] for q in range(4)], axis=1)
    pack_ref[3:4, :] = jnp.concatenate(
        [species_ref[q : q + 1, :] for q in range(4)], axis=1
    ).astype(F32)
    for n in (3,):
        fetches[n].wait()
    species = pack_ref[3:4, :]
    inv_root = by_species(species, [1.0 / math.sqrt(m) for m in MASSES])
    root = by_species(species, [math.sqrt(m) for m in MASSES])
    probes = [flat(probes_ref, 4 * j, PROBES, 12) for j in range(3)]
    start = [p * inv_root for p in probes]

    pl.semaphore_wait(barrier, len(partners))

    def copy(src, dst, sems, number, axis, by):
        return pltpu.make_async_remote_copy(
            src_ref=src,
            dst_ref=dst,
            send_sem=sems.at[0, number],
            recv_sem=sems.at[1, number],
            device_id={AXES[axis]: partner(axis, by)},
            device_id_type=MESH,
        )

    def tile(n):
        return pl.ds(8 * n, 8)

    def halo_start(send, recv, sems, axis, arrays):
        for n, value in enumerate(arrays):
            send[axis, tile(n), :] = value
        rows = pl.ds(0, 8 * len(arrays))
        copies = [
            copy(send.at[axis, rows], recv.at[axis, d, rows], sems, 2 * axis + d, axis, 1 - 2 * d)
            for d in (0, 1)
        ]
        for c in copies:
            c.start()
        return copies

    def halo_finish(recv, axis, copies, count):
        for c in copies:
            c.wait()
        return [
            lanes.merge(axis, recv[axis, 1, tile(n), :], recv[axis, 0, tile(n), :])
            for n in range(count)
        ]

    geometry = {(0, 0): [pack_ref[0:8, :]]}
    geo = (geo_send, geo_recv, geo_sems)
    halo = (halo_send, halo_recv, halo_sems)
    copies = halo_start(*geo, 1, geometry[0, 0])
    halo_copies = halo_start(*halo, 1, start)

    for n in (4, 5, 6, 7, 8, 2):
        fetches[n].wait()
    for s in range(3):
        acc_ref[pl.ds(64 * s, 64), :] = w2_ref[...] * emb_ref[s : s + 1, :]
    to_node = jnp.dot(
        acc_ref[...], wn_ref[...], precision=HIGHEST, preferred_element_type=F32
    ) * NORM_SCALE
    flipped = [jnp.transpose(to_node[64 * s : 64 * s + 64, :]) for s in range(3)]
    flip = [high_low(f) for f in flipped]
    left_node = jnp.concatenate(
        [jnp.concatenate([hi, hi, lo], axis=1) for hi, lo in flip], axis=0
    ).astype(BF16)
    first_high, first_low = high_low(w1_ref[...] * math.sqrt(2.0 / CUTOFF))
    left_radial = jnp.transpose(
        jnp.concatenate([first_high, first_high, first_low, jnp.zeros_like(first_high)], axis=0)
    ).astype(BF16)
    small_ref[0:8, :] = jnp.zeros((8, LANES), F32)
    small_ref[0:3, :] = emb_ref[...]
    small_ref[3:4, :] = readout_ref[...]
    columns = jnp.transpose(small_ref[0:8, :])
    readout = columns[:, 3:4]

    row_lane = lax.broadcasted_iota(jnp.int32, (32, LANES), 1)
    home = (
        ((row_lane >> 6) + 1) * (4 * 34) + (((row_lane >> 5) & 1) + 1) * 34 + (row_lane & 31) + 1
    )
    off = flat(index_ref, 0, 32, 4) - home

    def unit(value, bound):
        return jnp.where(value > bound, 1, 0) - jnp.where(value < -bound, 1, 0)

    off_x = unit(off, 68)
    rest = off - 136 * off_x
    off_y = unit(rest, 17)
    off_z = rest - 34 * off_y
    code = (off_x + 1) * 9 + (off_y + 1) * 3 + off_z + 1
    bits = jnp.where(off == 0, 0, jnp.left_shift(jnp.ones_like(code), code))
    bits = jnp.sum(bits, axis=0, keepdims=True)

    geometry[0, 1] = halo_finish(geo_recv, 1, copies, 1)
    copies = halo_start(*geo, 0, geometry[0, 0] + geometry[0, 1])
    y_old = {(0, 0): start}
    y_old[0, 1] = halo_finish(halo_recv, 1, halo_copies, 3)
    ghosts = halo_finish(geo_recv, 0, copies, 2)
    geometry[1, 0], geometry[1, 1] = [ghosts[0]], [ghosts[1]]
    copies = halo_start(*geo, 2, [geometry[k][0] for k in SITES])
    halo_copies = halo_start(*halo, 0, y_old[0, 0] + y_old[0, 1])

    for n, c in enumerate(CODES):
        rows_ref[9, pl.ds(n, 1), :] = (jnp.right_shift(bits, c) & 1).astype(F32)

    def edges_of(seen, count):
        for n in range(count):
            geo_ref[tile(n), :] = seen[CODES[n]][0]
        code_row = lax.broadcasted_iota(jnp.int32, (count, LANES), 0)
        if count == FLAT:
            number = code_row + jnp.where(code_row >= 4, 1, 0)
            offs = (number // 3, number % 3, jnp.ones_like(number))
        else:
            number = code_row + jnp.where(code_row >= 4, 1, 0)
            pair = (code_row - FLAT) // 2
            flat = code_row < FLAT
            offs = (
                jnp.where(flat, number // 3, pair // 3),
                jnp.where(flat, number % 3, pair % 3),
                jnp.where(flat, 1, 2 * (code_row % 2)),
            )
        vectors = [
            (off - 1).astype(F32) * SPACING
            + geo_ref[pl.ds(j, count, stride=8), :]
            - pack_ref[j : j + 1, :]
            for j, off in enumerate(offs)
        ]
        filled = rows_ref[9, 0:count, :]
        present = filled > 0.5
        square = vectors[0] * vectors[0] + vectors[1] * vectors[1] + vectors[2] * vectors[2]
        distance = jnp.sqrt(jnp.where(present, square, 1.0))
        inverse = 1.0 / distance
        part = distance * (1.0 / CUTOFF)
        part_sq = part * part
        for j in range(3):
            rows_ref[j, 0:count, :] = vectors[j] * inverse
        rows_ref[3, 0:count, :] = inverse
        rows_ref[4, 0:count, :] = filled * (1.0 - part_sq) * (1.0 - part_sq)
        rows_ref[5, 0:count, :] = filled * (-4.0 / CUTOFF) * part * (1.0 - part_sq)
        rows_ref[6, 0:count, :] = filled * (-4.0 / CUTOFF**2) * (1.0 - 3.0 * part_sq)
        rows_ref[7, 0:count, :] = geo_ref[pl.ds(3, count, stride=8), :]
        sin_1, cos_1 = sin_cos(distance * (math.pi / CUTOFF))
        sin_k, cos_k = sin_1, cos_1
        sin_b, cos_b = jnp.zeros_like(sin_1), jnp.ones_like(cos_1)
        for k in range(8):
            omega = (k + 1) * math.pi / CUTOFF
            trig_ref[pl.ds(k, count, stride=24), :] = sin_k
            trig_ref[pl.ds(8 + k, count, stride=24), :] = cos_k * omega
            trig_ref[pl.ds(16 + k, count, stride=24), :] = sin_k * (-omega * omega)
            sin_k, sin_b = 2.0 * cos_1 * sin_k - sin_b, sin_k
            cos_k, cos_b = 2.0 * cos_1 * cos_k - cos_b, cos_k

    edges_of(gather(lanes, {k: v + v for k, v in geometry.items()}, True), FLAT)

    acc_ref[...] = jnp.zeros_like(acc_ref)

    def radial(pair, carry):
        blocks = []
        for i in (0, 1):
            for g in range(3):
                hi, lo = high_low(trig_ref[pl.ds((2 * pair + i) * 24 + 8 * g, 8), :])
                blocks.append(jnp.concatenate([hi, lo, hi, jnp.zeros_like(hi)], axis=0))
        right = jnp.concatenate(blocks, axis=1).astype(BF16)
        waves = jnp.dot(left_radial, right, preferred_element_type=F32)
        rights = []
        for i in (0, 1):
            n = 2 * pair + i
            wave = [waves[:, 128 * (3 * i + g) : 128 * (3 * i + g + 1)] for g in range(3)]
            inv = rows_ref[3, pl.ds(n, 1), :]
            env = [rows_ref[4 + g, pl.ds(n, 1), :] for g in range(3)]
            kind = rows_ref[7, pl.ds(n, 1), :]
            x_0 = wave[0] * inv
            x_1 = (wave[1] - x_0) * inv
            x_2 = (wave[2] - 2.0 * x_1) * inv
            gate = 1.0 / (1.0 + jnp.exp(-x_0))
            shut = 1.0 - gate
            value = x_0 * gate
            slope = gate + value * shut
            bend = shut * (2.0 * gate + value * (1.0 - 2.0 * gate))
            r_1 = slope * x_1
            r_2 = bend * x_1 * x_1 + slope * x_2
            h_0 = value * env[0]
            h_1 = r_1 * env[0] + value * env[1]
            h_2 = r_2 * env[0] + 2.0 * r_1 * env[1] + value * env[2]
            second_ref[n] = h_2
            for s in range(3):
                one = jnp.where(jnp.abs(kind - s) < 0.5, 1.0, 0.0)
                acc_ref[pl.ds(64 * s, 64), :] += h_0 * one
            hi, lo = high_low(h_1)
            rights.append(jnp.concatenate([hi, lo, hi], axis=0).astype(BF16))
        product = jnp.dot(
            left_node, jnp.concatenate(rights, axis=1), preferred_element_type=F32
        )
        for i in (0, 1):
            n = 2 * pair + i
            kind = rows_ref[7, pl.ds(n, 1), :]
            cols = slice(128 * i, 128 * i + 128)
            prod_ref[n] = by_species(
                kind, [product[128 * s : 128 * s + 128, cols] for s in range(3)]
            )
        return carry

    lax.fori_loop(0, FLAT // 2, radial, 0, unroll=True)
    ghosts = halo_finish(geo_recv, 2, copies, 4)
    for n, k in enumerate(SITES):
        geometry[k] = geometry[k] + [ghosts[n]]
    edges_of(gather(lanes, geometry), NC)
    ghosts = halo_finish(halo_recv, 0, halo_copies, 6)
    y_old[1, 0], y_old[1, 1] = ghosts[:3], ghosts[3:]
    halo_copies = halo_start(*halo, 2, [lanes.pack(y_old[k]) for k in SITES])
    lax.fori_loop(FLAT // 2, NC // 2, radial, 0, unroll=True)

    home_kind = jnp.where(
        lax.broadcasted_iota(jnp.int32, (8, LANES), 0).astype(F32) == species, 1.0, 0.0
    )
    home_kind = jnp.where(lax.broadcasted_iota(jnp.int32, (8, LANES), 0) < 3, home_kind, 0.0)
    node = jnp.dot(columns, home_kind, precision=HIGHEST, preferred_element_type=F32)
    node = node + jnp.dot(
        jnp.concatenate(flipped, axis=1), acc_ref[...], precision=HIGHEST, preferred_element_type=F32
    )
    gate = 1.0 / (1.0 + jnp.exp(-node))
    shut = 1.0 - gate
    value = node * gate
    node_slope = readout * (gate + value * shut)
    node_ref[0] = node_slope
    node_ref[1] = readout * (shut * (2.0 * gate + value * (1.0 - 2.0 * gate)))
    acc_ref[...] = jnp.dot(to_node, node_slope, precision=HIGHEST, preferred_element_type=F32)

    def edge_terms(n, carry):
        mine = prod_ref[n]
        kind = rows_ref[7, pl.ds(n, 1), :]
        pull = jnp.sum(mine * node_ref[0], axis=0, keepdims=True) * rows_ref[3, pl.ds(n, 1), :]
        back = by_species(kind, [acc_ref[64 * s : 64 * s + 64, :] for s in range(3)])
        curve = jnp.sum(back * second_ref[n], axis=0, keepdims=True)
        rows_ref[8, pl.ds(n, 1), :] = pull
        rows_ref[10, pl.ds(n, 1), :] = curve - pull
        return carry

    lax.fori_loop(0, NC, edge_terms, 0)
    for low, high in BLOCKS:

        def edge_matrix(n, carry, low=low, high=high):
            bent = prod_ref[n] * node_ref[1]
            for m in range(high):
                both = jnp.sum(bent * prod_ref[m], axis=0, keepdims=True)
                both = jnp.broadcast_to(both, (8, LANES))
                matrix_ref[n * NC + m] = both
                if m < low:
                    matrix_ref[m * NC + n] = both
            matrix_ref[n * NC + n] = matrix_ref[n * NC + n] + rows_ref[10, pl.ds(n, 1), :]
            return carry

        lax.fori_loop(low, high, edge_matrix, 0)

    ghosts = halo_finish(halo_recv, 2, halo_copies, 4)
    for n, k in enumerate(SITES):
        y_old[k] = y_old[k] + [ghosts[n]]
    scale = 1.0 / radius_ref[0]
    weight_sq = {}
    for k in SITES:
        own, ghost = [
            by_species(g[3:4, :], [1.0 / m for m in MASSES]) * scale + jnp.zeros((8, LANES), F32)
            for g in geometry[k]
        ]
        weight_sq[k] = [own] * 3 + [lanes.pack([ghost] * 3)]

    def local_product(y):
        views = gather(lanes, y)
        for n, c in enumerate(CODES):
            total = jnp.zeros((8, LANES), F32)
            for j in range(3):
                change = views[c][j] - views[13][j]
                dv_ref[3 * n + j] = change
                total = total + rows_ref[j, n : n + 1, :] * change
            dr_ref[n] = total

        def force(n, carry):
            total = matrix_ref[n * NC] * dr_ref[0]
            for m in range(1, NC):
                total = total + matrix_ref[n * NC + m] * dr_ref[m]
            pull = rows_ref[8, pl.ds(n, 1), :]
            out, work = [], carry[3]
            for j in range(3):
                change = dv_ref[3 * n + j]
                edge = rows_ref[j, pl.ds(n, 1), :] * total + pull * change
                edge_ref[3 * n + j] = edge
                out.append(carry[j] - edge)
                work = work + edge * change
            return tuple(out) + (work,)

        zero = jnp.zeros((8, LANES), F32)
        centre = lax.fori_loop(0, NC, force, (zero,) * 4, unroll=2)
        terms = scatter(
            lanes, lambda c, j: centre[j] if c == 13 else edge_ref[3 * ORDER[c] + j]
        )
        return terms, centre[3] * scale

    def exchange(number, held, own_only, beside):
        for axis in (1, 0, 2):
            if axis < 2:
                owns = [k for k in SITES if k in held and k[axis] == 0]
                others = [(1, k[1]) if axis == 0 else (k[0], 1) for k in owns]
                own = [v for k in owns for v in held[k]]
                ghost = [v for k in others for v in held[k]]
            else:
                owns = [k for k in SITES if k in held]
                own = [lanes.pack(held[k][:3]) for k in owns]
                ghost = [held[k][3] for k in owns]
            for n in range(len(own)):
                fold_send[number, axis, 0, tile(n), :] = lanes.merge(axis, ghost[n], own[n])
                fold_send[number, axis, 1, tile(n), :] = lanes.merge(axis, own[n], ghost[n])
            rows = pl.ds(0, 8 * len(own))
            copies = [
                copy(
                    fold_send.at[number, axis, d, rows],
                    fold_recv.at[number, axis, d, rows],
                    fold_sems.at[number],
                    2 * axis + d,
                    axis,
                    1 - 2 * d,
                )
                for d in (0, 1)
            ]
            for c in copies:
                c.start()
            beside(axis)
            for c in copies:
                c.wait()
            below = [fold_recv[number, axis, 0, tile(n), :] for n in range(len(own))]
            above = [fold_recv[number, axis, 1, tile(n), :] for n in range(len(own))]
            to_own = [lanes.merge(axis, b, a) for b, a in zip(below, above)]
            to_ghost = [lanes.merge(axis, a, b) for b, a in zip(below, above)]
            after = {}
            for n, key in enumerate(owns):
                if axis < 2:
                    part = slice(4 * n, 4 * n + 4)
                    after[key] = [h + t for h, t in zip(held[key], to_own[part])]
                    if not own_only:
                        other = others[n]
                        after[other] = [h + t for h, t in zip(held[other], to_ghost[part])]
                else:
                    more = lanes.unpack(to_own[n], 3)
                    after[key] = [h + t for h, t in zip(held[key][:3], more)]
                    after[key].append(held[key][3] + to_ghost[n])
            held = after
        return held

    def sum_start(axis):
        sum_send[axis] = moments_ref[...]
        copies = []
        for by in range(1, sizes[axis]):
            c = copy(
                sum_send.at[axis],
                sum_recv.at[axis, by],
                sum_sems.at[axis],
                by,
                axis,
                by,
            )
            c.start()
            copies.append(c)
        return copies

    def sum_finish(axis, copies):
        for c in copies:
            c.wait()
        sum_recv[axis, 0] = sum_send[axis]
        total = jnp.zeros((8, LANES), F32)
        for index in range(sizes[axis]):
            slot = lax.rem(place[axis] + (sizes[axis] - index), sizes[axis])
            total = total + sum_recv[axis, slot]
        moments_ref[...] = total

    terms, work_1 = local_product(y_old)
    product = exchange(0, terms, False, lambda axis: None)
    y_1 = {k: [a * w for a, w in zip(product[k], weight_sq[k])] for k in SITES}
    t_1 = [y_1[0, 0][j] * root for j in range(3)]
    flight = {}

    def beside_second(axis):
        if axis == 1:
            square = sum(p * p for p in probes)
            parts = (
                square,
                work_1,
                2.0 * sum(t * t for t in t_1) - square,
                4.0 * work_2 - 3.0 * work_1,
            )
            packed = jnp.zeros((8, LANES), F32)
            for k in range(4):
                total = jnp.sum(parts[k], axis=1, keepdims=True)
                packed = jnp.where(lanes.lane == k, total, packed)
            moments_ref[...] = packed
            flight[0] = sum_start(0)
        if axis == 2:
            sum_finish(0, flight.pop(0))
            flight[1] = sum_start(1)

    terms, work_2 = local_product(y_1)
    product = exchange(1, terms, False, beside_second)
    y_2 = {
        k: [2.0 * a * w - o for a, w, o in zip(product[k], weight_sq[k], y_old[k])] for k in SITES
    }
    terms, unused = local_product(y_2)

    def spread(which, j, value):
        for q in range(4):
            part = value if q == 0 else roll(value, -32 * q)
            cheb_ref[pl.ds(96 * which + 4 * j + q, PROBES, stride=12), :] = part[:, 0:32]

    def beside_third(axis):
        if axis == 1:
            for j in range(3):
                spread(0, j, y_2[0, 0][j] * root)
            sum_finish(1, flight.pop(1))
            flight[2] = sum_start(2)

    product = exchange(2, terms, True, beside_third)
    for j in range(3):
        spread(1, j, 2.0 * product[0, 0][j] * weight_sq[0, 0][j] * root - t_1[j])
    sum_finish(2, flight.pop(2))
    result_ref[...] = jnp.transpose(moments_ref[...])[0:4, :]


def on_device(
    sizes,
    displacements,
    species,
    neighbor_index,
    probes,
    embedding,
    w_radial1,
    w_radial2,
    w_node,
    readout,
    spectral_radius,
):
    vmem = pl.BlockSpec(memory_space=pltpu.VMEM)
    most = max(sizes)
    operands = (
        displacements.reshape(3, 4, 32),
        species.reshape(-1, 32),
        neighbor_index.reshape(-1, 32),
        probes.reshape(-1, 32),
        embedding,
        w_radial1,
        w_radial2,
        w_node,
        readout.reshape(1, -1),
    )
    cheb, result = pl.pallas_call(
        functools.partial(kernel, sizes),
        out_shape=(
            jax.ShapeDtypeStruct((24 * PROBES, 32), F32),
            jax.ShapeDtypeStruct((4, PROBES), F32),
        ),
        in_specs=[pl.BlockSpec(memory_space=pltpu.SMEM)] + [pl.BlockSpec(memory_space=pl.ANY)] * 9,
        out_specs=(vmem, vmem),
        scratch_shapes=[
            pltpu.VMEM((8, LANES), F32),
            pltpu.VMEM((3, 32, LANES), F32),
            pltpu.VMEM((3, 2, 32, LANES), F32),
            pltpu.VMEM((3, 48, LANES), F32),
            pltpu.VMEM((3, 2, 48, LANES), F32),
            pltpu.VMEM((3, 3, 2, 64, LANES), F32),
            pltpu.VMEM((3, 3, 2, 64, LANES), F32),
            pltpu.VMEM((3, 8, LANES), F32),
            pltpu.VMEM((3, most, 8, LANES), F32),
            pltpu.SemaphoreType.DMA((2, 6)),
            pltpu.SemaphoreType.DMA((2, 6)),
            pltpu.SemaphoreType.DMA((3, 2, 6)),
            pltpu.SemaphoreType.DMA((3, 2, most)),
            pltpu.VMEM((8 * NC, LANES), F32),
            pltpu.VMEM((24 * NC, LANES), F32),
            pltpu.VMEM((11, 32, LANES), F32),
            pltpu.VMEM((3 * HID, LANES), F32),
            pltpu.VMEM((NC, 128, LANES), F32),
            pltpu.VMEM((NC, HID, LANES), F32),
            pltpu.VMEM((2, 128, LANES), F32),
            pltpu.VMEM((NC * NC, 8, LANES), F32),
            pltpu.VMEM((3 * NC, 8, LANES), F32),
            pltpu.VMEM((NC, 8, LANES), F32),
            pltpu.VMEM((3 * NC, 8, LANES), F32),
            pltpu.VMEM((8, LANES), F32),
            pltpu.VMEM((8, LANES), F32),
        ]
        + [pltpu.VMEM(v.shape, v.dtype) for v in operands]
        + [pltpu.SemaphoreType.DMA((len(operands),))],
        compiler_params=pltpu.CompilerParams(
            collective_id=0, has_side_effects=True, vmem_limit_bytes=60 * 2**20
        ),
        name="chebyshev",
    )(
        spectral_radius,
        *operands,
    )
    return cheb.reshape((2,) + probes.shape), result


def solution(mesh):
    placed = (
        P(None, "gx", "gy", "gz"),
        P("gx", "gy", "gz"),
        P(None, "gx", "gy", "gz"),
        P(None, None, "gx", "gy", "gz"),
        P(),
        P(),
        P(),
        P(),
        P(),
        P(),
    )
    return jax.shard_map(
        functools.partial(on_device, tuple(mesh.shape[axis] for axis in AXES)),
        mesh=mesh,
        in_specs=placed,
        out_specs=(P(None, None, None, "gx", "gy", "gz"), P()),
        check_vma=False,
    )
```

```python
import functools
import math

import jax
import jax.numpy as jnp
from jax import lax
from jax.experimental import pallas as pl
from jax.experimental.pallas import tpu as pltpu
from jax.sharding import PartitionSpec as P

SPACING = 2.2
CUTOFF = 5.0
NORM_SCALE = 0.22360679774997896
MASSES = (28.0855, 15.999, 22.99)
HIGHEST = lax.Precision.HIGHEST
MESH = pl.DeviceIdType.MESH
F32 = jnp.float32
BF16 = jnp.bfloat16

CODES = tuple(sorted((c for c in range(27) if c != 13), key=lambda c: (c % 3 != 1, c)))
ORDER = {c: n for n, c in enumerate(CODES)}
NC = len(CODES)
FLAT = 8
WAYS = tuple(
    sorted(
        (
            (x, y, z)
            for x in (-1, 0, 1)
            for y in (-1, 0, 1)
            for z in (-1, 0, 1)
            if (x, y, z) != (0, 0, 0)
        ),
        key=lambda way: (way[2] == 0, -sum(map(abs, way))),
    )
)
BLOCKS = ((0, 7), (7, 14), (14, 20), (20, 26))
AXES = ("gx", "gy", "gz")
LANES = 128
HID = 64
PROBES = 8


def roll(value, by):
    return pltpu.roll(value, by % LANES, 1)


def high_low(value):
    high = value.astype(BF16).astype(F32)
    return high, value - high


def by_species(species, values):
    return jnp.where(species < 0.5, values[0], jnp.where(species < 1.5, values[1], values[2]))


def sin_cos(angle):
    off = angle - math.pi / 2
    square = off * off
    odd = jnp.full_like(off, -1.0 / math.factorial(15))
    for power in (13, 11, 9, 7, 5, 3, 1):
        odd = odd * square + (-1.0) ** (power // 2) / math.factorial(power)
    even = jnp.full_like(off, 1.0 / math.factorial(16))
    for power in (14, 12, 10, 8, 6, 4, 2, 0):
        even = even * square + (-1.0) ** (power // 2) / math.factorial(power)
    return even, -odd * off


class Lanes:
    def __init__(self):
        lane = lax.broadcasted_iota(jnp.int32, (8, LANES), 1)
        self.lane = lane
        self.upper = (lane >= 64, (lane & 32) != 0)
        self.z = lane & 31
        self.low_z = self.z < 16
        self.outer = (self.z < 3) | (self.z > 28)
        self.first = [self.z == j for j in range(3)]
        self.last = [self.z == 31 - j for j in range(3)]

    def swap(self, axis, value):
        if axis == 0:
            return roll(value, 64)
        return jnp.where(self.upper[1], roll(value, 32), roll(value, -32))

    def merge(self, axis, low_value, high_value):
        if axis < 2:
            return jnp.where(self.upper[axis], high_value, low_value)
        return jnp.where(self.low_z, low_value, high_value)

    def ends(self, low_values, high_values):
        out = jnp.zeros((8, LANES), F32)
        for j, (low, high) in enumerate(zip(low_values, high_values)):
            out = jnp.where(self.first[j], low, jnp.where(self.last[j], high, out))
        return out

    def pack(self, values):
        return self.ends(
            [roll(v, j) if j else v for j, v in enumerate(values)],
            [roll(v, -j) if j else v for j, v in enumerate(values)],
        )

    def unpack(self, packed, count):
        out = []
        for j in range(count):
            low, high = (roll(packed, -j), roll(packed, j)) if j else (packed, packed)
            out.append(jnp.where(self.first[0], low, jnp.where(self.last[0], high, 0.0)))
        return out


SITES = tuple((gx, gy) for gx in (0, 1) for gy in (0, 1))


def gather(lanes, ext, flat_only=False):
    count = len(ext[0, 0]) - 1
    along_x = {}
    for gy in (0, 1):
        own, ghost = ext[0, gy], ext[1, gy]
        along_x[0, gy] = own
        along_x[1, gy] = [lanes.swap(0, lanes.merge(0, g, o)) for o, g in zip(own, ghost)]
        along_x[-1, gy] = [lanes.swap(0, lanes.merge(0, o, g)) for o, g in zip(own, ghost)]
    out = {}
    for sx in (-1, 0, 1):
        own, ghost = along_x[sx, 0], along_x[sx, 1]
        along_y = {
            0: own,
            1: [lanes.swap(1, lanes.merge(1, g, o)) for o, g in zip(own, ghost)],
            -1: [lanes.swap(1, lanes.merge(1, o, g)) for o, g in zip(own, ghost)],
        }
        for sy in (-1, 0, 1):
            values, packed = along_y[sy][:count], along_y[sy][count]
            base = (sx + 1) * 9 + (sy + 1) * 3 + 1
            out[base] = values
            if flat_only:
                continue
            out[base + 1] = [
                jnp.where(lanes.last[0], roll(packed, 31 - j), roll(v, -1))
                for j, v in enumerate(values)
            ]
            out[base - 1] = [
                jnp.where(lanes.first[0], roll(packed, j - 31), roll(v, 1))
                for j, v in enumerate(values)
            ]
    return out


def scatter(lanes, edges):
    along_z = {}
    for sx in (-1, 0, 1):
        for sy in (-1, 0, 1):
            base = (sx + 1) * 9 + (sy + 1) * 3 + 1
            values, lows, highs = [], [], []
            for j in range(3):
                up, down = edges(base + 1, j), edges(base - 1, j)
                own = edges(base, j)
                own = own + jnp.where(lanes.first[0], 0.0, roll(up, 1))
                values.append(own + jnp.where(lanes.last[0], 0.0, roll(down, -1)))
                lows.append(roll(up, j - 31))
                highs.append(roll(down, 31 - j))
            along_z[sx, sy] = values + [lanes.ends(lows, highs)]
    along_y = {}
    for sx in (-1, 0, 1):
        items = list(zip(along_z[sx, -1], along_z[sx, 0], along_z[sx, 1]))
        along_y[sx, 0] = [m + lanes.swap(1, lanes.merge(1, up, down)) for down, m, up in items]
        along_y[sx, 1] = [lanes.swap(1, lanes.merge(1, down, up)) for down, m, up in items]
    ext = {}
    for gy in (0, 1):
        items = list(zip(along_y[-1, gy], along_y[0, gy], along_y[1, gy]))
        ext[0, gy] = [m + lanes.swap(0, lanes.merge(0, up, down)) for down, m, up in items]
        ext[1, gy] = [lanes.swap(0, lanes.merge(0, down, up)) for down, m, up in items]
    return ext


def kernel(
    sizes,
    radius_ref,
    *refs,
):
    sources, refs = refs[:9], refs[9:]
    (
        cheb_ref,
        result_ref,
        moments_ref,
        geo_send,
        geo_recv,
        halo_send,
        halo_recv,
        fold_send,
        fold_recv,
        sum_send,
        sum_recv,
        geo_sems,
        halo_sems,
        fold_sems,
        sum_sems,
        geo_ref,
        trig_ref,
        rows_ref,
        acc_ref,
        prod_ref,
        second_ref,
        node_ref,
        matrix_ref,
        dv_ref,
        dr_ref,
        edge_ref,
        small_ref,
        pack_ref,
    ) = refs[: -10]
    fetched, fetch_sems = refs[-10:-1], refs[-1]
    disp_ref, species_ref, index_ref, probes_ref, emb_ref, w1_ref, w2_ref, wn_ref, readout_ref = fetched
    fetches = [
        pltpu.make_async_copy(src, dst, fetch_sems.at[n])
        for n, (src, dst) in enumerate(zip(sources, fetched))
    ]
    for n in (0, 1, 3, 4, 5, 6, 7, 8, 2):
        fetches[n].start()

    place = [lax.axis_index(axis) for axis in AXES]

    def partner(axis, by):
        return lax.rem(place[axis] + (by + sizes[axis]), sizes[axis])

    barrier = pltpu.get_barrier_semaphore()
    partners = [(axis, by) for axis in range(3) for by in range(1, sizes[axis])]
    for axis, by in partners:
        pl.semaphore_signal(
            barrier, inc=1, device_id={AXES[axis]: partner(axis, by)}, device_id_type=MESH
        )

    def flat(ref, first, count, stride):
        return jnp.concatenate(
            [ref[pl.ds(first + q, count, stride=stride), :] for q in range(4)], axis=1
        )

    lanes = Lanes()
    pack_ref[0:8, :] = jnp.zeros((8, LANES), F32)
    for n in (0, 1):
        fetches[n].wait()
    pack_ref[0:3, :] = jnp.concatenate([disp_ref[:, q, :] for q in range(4)], axis=1)
    pack_ref[3:4, :] = jnp.concatenate(
        [species_ref[q : q + 1, :] for q in range(4)], axis=1
    ).astype(F32)
    for n in (3,):
        fetches[n].wait()
    species = pack_ref[3:4, :]
    inv_root = by_species(species, [1.0 / math.sqrt(m) for m in MASSES])
    root = by_species(species, [math.sqrt(m) for m in MASSES])
    probes = [flat(probes_ref, 4 * j, PROBES, 12) for j in range(3)]
    start = [p * inv_root for p in probes]

    pl.semaphore_wait(barrier, len(partners))

    def copy(src, dst, sems, number, axis, by):
        return pltpu.make_async_remote_copy(
            src_ref=src,
            dst_ref=dst,
            send_sem=sems.at[0, number],
            recv_sem=sems.at[1, number],
            device_id={AXES[axis]: partner(axis, by)},
            device_id_type=MESH,
        )

    def tile(n):
        return pl.ds(8 * n, 8)

    def halo_start(send, recv, sems, axis, arrays):
        for n, value in enumerate(arrays):
            send[axis, tile(n), :] = value
        rows = pl.ds(0, 8 * len(arrays))
        copies = [
            copy(send.at[axis, rows], recv.at[axis, d, rows], sems, 2 * axis + d, axis, 1 - 2 * d)
            for d in (0, 1)
        ]
        for c in copies:
            c.start()
        return copies

    def halo_finish(recv, axis, copies, count):
        for c in copies:
            c.wait()
        return [
            lanes.merge(axis, recv[axis, 1, tile(n), :], recv[axis, 0, tile(n), :])
            for n in range(count)
        ]

    geometry = {(0, 0): [pack_ref[0:8, :]]}
    geo = (geo_send, geo_recv, geo_sems)
    halo = (halo_send, halo_recv, halo_sems)
    copies = halo_start(*geo, 1, geometry[0, 0])
    halo_copies = halo_start(*halo, 1, start)

    for n in (4, 5, 6, 7, 8, 2):
        fetches[n].wait()
    for s in range(3):
        acc_ref[pl.ds(64 * s, 64), :] = w2_ref[...] * emb_ref[s : s + 1, :]
    to_node = jnp.dot(
        acc_ref[...], wn_ref[...], precision=HIGHEST, preferred_element_type=F32
    ) * NORM_SCALE
    flipped = [jnp.transpose(to_node[64 * s : 64 * s + 64, :]) for s in range(3)]
    flip = [high_low(f) for f in flipped]
    left_node = jnp.concatenate(
        [jnp.concatenate([hi, hi, lo], axis=1) for hi, lo in flip], axis=0
    ).astype(BF16)
    first_high, first_low = high_low(w1_ref[...] * math.sqrt(2.0 / CUTOFF))
    left_radial = jnp.transpose(
        jnp.concatenate([first_high, first_high, first_low, jnp.zeros_like(first_high)], axis=0)
    ).astype(BF16)
    small_ref[0:8, :] = jnp.zeros((8, LANES), F32)
    small_ref[0:3, :] = emb_ref[...]
    small_ref[3:4, :] = readout_ref[...]
    columns = jnp.transpose(small_ref[0:8, :])
    readout = columns[:, 3:4]

    row_lane = lax.broadcasted_iota(jnp.int32, (32, LANES), 1)
    home = (
        ((row_lane >> 6) + 1) * (4 * 34) + (((row_lane >> 5) & 1) + 1) * 34 + (row_lane & 31) + 1
    )
    off = flat(index_ref, 0, 32, 4) - home

    def unit(value, bound):
        return jnp.where(value > bound, 1, 0) - jnp.where(value < -bound, 1, 0)

    off_x = unit(off, 68)
    rest = off - 136 * off_x
    off_y = unit(rest, 17)
    off_z = rest - 34 * off_y
    code = (off_x + 1) * 9 + (off_y + 1) * 3 + off_z + 1
    bits = jnp.where(off == 0, 0, jnp.left_shift(jnp.ones_like(code), code))
    bits = jnp.sum(bits, axis=0, keepdims=True)

    geometry[0, 1] = halo_finish(geo_recv, 1, copies, 1)
    copies = halo_start(*geo, 0, geometry[0, 0] + geometry[0, 1])
    y_old = {(0, 0): start}
    y_old[0, 1] = halo_finish(halo_recv, 1, halo_copies, 3)
    ghosts = halo_finish(geo_recv, 0, copies, 2)
    geometry[1, 0], geometry[1, 1] = [ghosts[0]], [ghosts[1]]
    copies = halo_start(*geo, 2, [geometry[k][0] for k in SITES])
    halo_copies = halo_start(*halo, 0, y_old[0, 0] + y_old[0, 1])

    for n, c in enumerate(CODES):
        rows_ref[9, pl.ds(n, 1), :] = (jnp.right_shift(bits, c) & 1).astype(F32)

    def edges_of(seen, count):
        for n in range(count):
            geo_ref[tile(n), :] = seen[CODES[n]][0]
        code_row = lax.broadcasted_iota(jnp.int32, (count, LANES), 0)
        if count == FLAT:
            number = code_row + jnp.where(code_row >= 4, 1, 0)
            offs = (number // 3, number % 3, jnp.ones_like(number))
        else:
            number = code_row + jnp.where(code_row >= 4, 1, 0)
            pair = (code_row - FLAT) // 2
            flat = code_row < FLAT
            offs = (
                jnp.where(flat, number // 3, pair // 3),
                jnp.where(flat, number % 3, pair % 3),
                jnp.where(flat, 1, 2 * (code_row % 2)),
            )
        vectors = [
            (off - 1).astype(F32) * SPACING
            + geo_ref[pl.ds(j, count, stride=8), :]
            - pack_ref[j : j + 1, :]
            for j, off in enumerate(offs)
        ]
        filled = rows_ref[9, 0:count, :]
        present = filled > 0.5
        square = vectors[0] * vectors[0] + vectors[1] * vectors[1] + vectors[2] * vectors[2]
        distance = jnp.sqrt(jnp.where(present, square, 1.0))
        inverse = 1.0 / distance
        part = distance * (1.0 / CUTOFF)
        part_sq = part * part
        for j in range(3):
            rows_ref[j, 0:count, :] = vectors[j] * inverse
        rows_ref[3, 0:count, :] = inverse
        rows_ref[4, 0:count, :] = filled * (1.0 - part_sq) * (1.0 - part_sq)
        rows_ref[5, 0:count, :] = filled * (-4.0 / CUTOFF) * part * (1.0 - part_sq)
        rows_ref[6, 0:count, :] = filled * (-4.0 / CUTOFF**2) * (1.0 - 3.0 * part_sq)
        rows_ref[7, 0:count, :] = geo_ref[pl.ds(3, count, stride=8), :]
        sin_1, cos_1 = sin_cos(distance * (math.pi / CUTOFF))
        sin_k, cos_k = sin_1, cos_1
        sin_b, cos_b = jnp.zeros_like(sin_1), jnp.ones_like(cos_1)
        for k in range(8):
            omega = (k + 1) * math.pi / CUTOFF
            trig_ref[pl.ds(k, count, stride=24), :] = sin_k
            trig_ref[pl.ds(8 + k, count, stride=24), :] = cos_k * omega
            trig_ref[pl.ds(16 + k, count, stride=24), :] = sin_k * (-omega * omega)
            sin_k, sin_b = 2.0 * cos_1 * sin_k - sin_b, sin_k
            cos_k, cos_b = 2.0 * cos_1 * cos_k - cos_b, cos_k

    edges_of(gather(lanes, {k: v + v for k, v in geometry.items()}, True), FLAT)

    acc_ref[...] = jnp.zeros_like(acc_ref)

    def radial(pair, carry):
        blocks = []
        for i in (0, 1):
            for g in range(3):
                hi, lo = high_low(trig_ref[pl.ds((2 * pair + i) * 24 + 8 * g, 8), :])
                blocks.append(jnp.concatenate([hi, lo, hi, jnp.zeros_like(hi)], axis=0))
        right = jnp.concatenate(blocks, axis=1).astype(BF16)
        waves = jnp.dot(left_radial, right, preferred_element_type=F32)
        rights = []
        for i in (0, 1):
            n = 2 * pair + i
            wave = [waves[:, 128 * (3 * i + g) : 128 * (3 * i + g + 1)] for g in range(3)]
            inv = rows_ref[3, pl.ds(n, 1), :]
            env = [rows_ref[4 + g, pl.ds(n, 1), :] for g in range(3)]
            kind = rows_ref[7, pl.ds(n, 1), :]
            x_0 = wave[0] * inv
            x_1 = (wave[1] - x_0) * inv
            x_2 = (wave[2] - 2.0 * x_1) * inv
            gate = 1.0 / (1.0 + jnp.exp(-x_0))
            shut = 1.0 - gate
            value = x_0 * gate
            slope = gate + value * shut
            bend = shut * (2.0 * gate + value * (1.0 - 2.0 * gate))
            r_1 = slope * x_1
            r_2 = bend * x_1 * x_1 + slope * x_2
            h_0 = value * env[0]
            h_1 = r_1 * env[0] + value * env[1]
            h_2 = r_2 * env[0] + 2.0 * r_1 * env[1] + value * env[2]
            second_ref[n] = h_2
            for s in range(3):
                one = jnp.where(jnp.abs(kind - s) < 0.5, 1.0, 0.0)
                acc_ref[pl.ds(64 * s, 64), :] += h_0 * one
            hi, lo = high_low(h_1)
            rights.append(jnp.concatenate([hi, lo, hi], axis=0).astype(BF16))
        product = jnp.dot(
            left_node, jnp.concatenate(rights, axis=1), preferred_element_type=F32
        )
        for i in (0, 1):
            n = 2 * pair + i
            kind = rows_ref[7, pl.ds(n, 1), :]
            cols = slice(128 * i, 128 * i + 128)
            prod_ref[n] = by_species(
                kind, [product[128 * s : 128 * s + 128, cols] for s in range(3)]
            )
        return carry

    lax.fori_loop(0, FLAT // 2, radial, 0, unroll=True)
    ghosts = halo_finish(geo_recv, 2, copies, 4)
    for n, k in enumerate(SITES):
        geometry[k] = geometry[k] + [ghosts[n]]
    edges_of(gather(lanes, geometry), NC)
    ghosts = halo_finish(halo_recv, 0, halo_copies, 6)
    y_old[1, 0], y_old[1, 1] = ghosts[:3], ghosts[3:]
    halo_copies = halo_start(*halo, 2, [lanes.pack(y_old[k]) for k in SITES])
    lax.fori_loop(FLAT // 2, NC // 2, radial, 0, unroll=True)

    home_kind = jnp.where(
        lax.broadcasted_iota(jnp.int32, (8, LANES), 0).astype(F32) == species, 1.0, 0.0
    )
    home_kind = jnp.where(lax.broadcasted_iota(jnp.int32, (8, LANES), 0) < 3, home_kind, 0.0)
    node = jnp.dot(columns, home_kind, precision=HIGHEST, preferred_element_type=F32)
    node = node + jnp.dot(
        jnp.concatenate(flipped, axis=1), acc_ref[...], precision=HIGHEST, preferred_element_type=F32
    )
    gate = 1.0 / (1.0 + jnp.exp(-node))
    shut = 1.0 - gate
    value = node * gate
    node_slope = readout * (gate + value * shut)
    node_ref[0] = node_slope
    node_ref[1] = readout * (shut * (2.0 * gate + value * (1.0 - 2.0 * gate)))
    acc_ref[...] = jnp.dot(to_node, node_slope, precision=HIGHEST, preferred_element_type=F32)

    def edge_terms(n, carry):
        mine = prod_ref[n]
        kind = rows_ref[7, pl.ds(n, 1), :]
        pull = jnp.sum(mine * node_ref[0], axis=0, keepdims=True) * rows_ref[3, pl.ds(n, 1), :]
        back = by_species(kind, [acc_ref[64 * s : 64 * s + 64, :] for s in range(3)])
        curve = jnp.sum(back * second_ref[n], axis=0, keepdims=True)
        rows_ref[8, pl.ds(n, 1), :] = pull
        rows_ref[10, pl.ds(n, 1), :] = curve - pull
        return carry

    lax.fori_loop(0, NC, edge_terms, 0)
    for low, high in BLOCKS:

        def edge_matrix(n, carry, low=low, high=high):
            bent = prod_ref[n] * node_ref[1]
            for m in range(high):
                both = jnp.sum(bent * prod_ref[m], axis=0, keepdims=True)
                both = jnp.broadcast_to(both, (8, LANES))
                matrix_ref[n * NC + m] = both
                if m < low:
                    matrix_ref[m * NC + n] = both
            matrix_ref[n * NC + n] = matrix_ref[n * NC + n] + rows_ref[10, pl.ds(n, 1), :]
            return carry

        lax.fori_loop(low, high, edge_matrix, 0)

    ghosts = halo_finish(halo_recv, 2, halo_copies, 4)
    for n, k in enumerate(SITES):
        y_old[k] = y_old[k] + [ghosts[n]]
    scale = 1.0 / radius_ref[0]
    weight_sq = {}
    for k in SITES:
        own, ghost = [
            by_species(g[3:4, :], [1.0 / m for m in MASSES]) * scale + jnp.zeros((8, LANES), F32)
            for g in geometry[k]
        ]
        weight_sq[k] = [own] * 3 + [lanes.pack([ghost] * 3)]

    def local_product(y):
        views = gather(lanes, y)
        for n, c in enumerate(CODES):
            total = jnp.zeros((8, LANES), F32)
            for j in range(3):
                change = views[c][j] - views[13][j]
                dv_ref[3 * n + j] = change
                total = total + rows_ref[j, n : n + 1, :] * change
            dr_ref[n] = total

        def force(n, carry):
            total = matrix_ref[n * NC] * dr_ref[0]
            for m in range(1, NC):
                total = total + matrix_ref[n * NC + m] * dr_ref[m]
            pull = rows_ref[8, pl.ds(n, 1), :]
            out, work = [], carry[3]
            for j in range(3):
                change = dv_ref[3 * n + j]
                edge = rows_ref[j, pl.ds(n, 1), :] * total + pull * change
                edge_ref[3 * n + j] = edge
                out.append(carry[j] - edge)
                work = work + edge * change
            return tuple(out) + (work,)

        zero = jnp.zeros((8, LANES), F32)
        centre = lax.fori_loop(0, NC, force, (zero,) * 4, unroll=2)
        terms = scatter(
            lanes, lambda c, j: centre[j] if c == 13 else edge_ref[3 * ORDER[c] + j]
        )
        return terms, centre[3] * scale

    def exchange(number, held, own_only, beside):
        count = 3 if own_only else 4

        def leaving(axis, sign, table):
            out = {}
            for k, own in table.items():
                if sign == 0:
                    if k[axis] == 0 or not own_only:
                        out[k] = own
                elif k[axis] == 0:
                    ghost = table[(1, k[1]) if axis == 0 else (k[0], 1)]
                    pairs = zip(ghost, own) if sign > 0 else zip(own, ghost)
                    out[k] = [lanes.merge(axis, low, high) for low, high in pairs]
            return out

        def arriving(axis, plus, minus):
            out = {}
            for k in plus:
                out[k] = [lanes.merge(axis, p, m) for p, m in zip(plus[k], minus[k])]
                if not own_only:
                    other = (1, k[1]) if axis == 0 else (k[0], 1)
                    out[other] = [lanes.merge(axis, m, p) for p, m in zip(plus[k], minus[k])]
            return out

        def joined(first, *others):
            return {
                k: [sum(o[k][n] for o in others) + v for n, v in enumerate(items)]
                for k, items in first.items()
            }

        def pair(first, second):
            moved = lanes.merge(2, roll(second, 3), roll(second, -3))
            return jnp.where(lanes.outer, first, moved)

        def second_of(both):
            return lanes.merge(2, roll(both, -3), roll(both, 3))

        layers = {0: {k: v[:count] for k, v in held.items()}}
        for sign in (1, -1):
            layers[sign] = {}
            for k, v in held.items():
                own = lanes.pack(v[:3])
                low, high = (v[3], own) if sign > 0 else (own, v[3])
                layers[sign][k] = [lanes.merge(2, low, high)]

        copies, keys = {}, {}
        for slot, way in enumerate(WAYS):
            table = leaving(1, way[1], leaving(0, way[0], layers[way[2]]))
            keys[way] = sorted(table)
            items = [v for k in keys[way] for v in table[k]]
            if way[2] and len(items) > 1:
                items = [pair(*items[n : n + 2]) for n in range(0, len(items), 2)]
            for n, v in enumerate(items):
                fold_send[number, slot, tile(n), :] = v
            rows = pl.ds(0, 8 * len(items))
            copies[way] = pltpu.make_async_remote_copy(
                src_ref=fold_send.at[number, slot, rows],
                dst_ref=fold_recv.at[number, slot, rows],
                send_sem=fold_sems.at[number, 0, slot],
                recv_sem=fold_sems.at[number, 1, slot],
                device_id=tuple(partner(axis, way[axis]) for axis in range(3)),
                device_id_type=MESH,
            )
            copies[way].start()
        beside()

        def arrived(*way):
            slot = WAYS.index(way)
            copies[way].wait_recv()
            count_of = count if way[2] == 0 else 1
            total = count_of * len(keys[way])
            if way[2] and total > 1:
                items = []
                for n in range(total // 2):
                    both = fold_recv[number, slot, tile(n), :]
                    items += [both, second_of(both)]
            else:
                items = [fold_recv[number, slot, tile(n), :] for n in range(total)]
            return {
                k: items[count_of * n : count_of * n + count_of] for n, k in enumerate(keys[way])
            }

        def plane(layer, centre):
            along_x = arriving(0, arrived(1, 0, layer), arrived(-1, 0, layer))
            sides = [
                joined(
                    arrived(0, s, layer),
                    arriving(0, arrived(1, s, layer), arrived(-1, s, layer)),
                )
                for s in (1, -1)
            ]
            return joined(centre, along_x, arriving(1, *sides))

        sites = SITES[:1] if own_only else SITES
        flat = plane(0, {k: layers[0][k] for k in sites})
        above = plane(1, arrived(0, 0, 1))
        below = plane(-1, arrived(0, 0, -1))
        out = {}
        for k in sites:
            more = lanes.unpack(lanes.merge(2, above[k][0], below[k][0]), 3)
            out[k] = [h + t for h, t in zip(flat[k][:3], more)]
            if not own_only:
                out[k].append(flat[k][3] + lanes.merge(2, below[k][0], above[k][0]))
        for c in copies.values():
            c.wait_send()
        return out

    def sum_start(axis):
        sum_send[axis] = moments_ref[...]
        copies = []
        for by in range(1, sizes[axis]):
            c = copy(
                sum_send.at[axis],
                sum_recv.at[axis, by],
                sum_sems.at[axis],
                by,
                axis,
                by,
            )
            c.start()
            copies.append(c)
        return copies

    def sum_finish(axis, copies):
        for c in copies:
            c.wait()
        sum_recv[axis, 0] = sum_send[axis]
        total = jnp.zeros((8, LANES), F32)
        for index in range(sizes[axis]):
            slot = lax.rem(place[axis] + (sizes[axis] - index), sizes[axis])
            total = total + sum_recv[axis, slot]
        moments_ref[...] = total

    terms, work_1 = local_product(y_old)
    product = exchange(0, terms, False, lambda: None)
    y_1 = {k: [a * w for a, w in zip(product[k], weight_sq[k])] for k in SITES}
    t_1 = [y_1[0, 0][j] * root for j in range(3)]
    flight = {}

    def beside_second():
        square = sum(p * p for p in probes)
        parts = (
            square,
            work_1,
            2.0 * sum(t * t for t in t_1) - square,
            4.0 * work_2 - 3.0 * work_1,
        )
        packed = jnp.zeros((8, LANES), F32)
        for k in range(4):
            total = jnp.sum(parts[k], axis=1, keepdims=True)
            packed = jnp.where(lanes.lane == k, total, packed)
        moments_ref[...] = packed
        flight[0] = sum_start(0)

    terms, work_2 = local_product(y_1)
    product = exchange(1, terms, False, beside_second)
    y_2 = {
        k: [2.0 * a * w - o for a, w, o in zip(product[k], weight_sq[k], y_old[k])] for k in SITES
    }
    sum_finish(0, flight.pop(0))
    flight[1] = sum_start(1)
    terms, unused = local_product(y_2)

    def spread(which, j, value):
        for q in range(4):
            part = value if q == 0 else roll(value, -32 * q)
            cheb_ref[pl.ds(96 * which + 4 * j + q, PROBES, stride=12), :] = part[:, 0:32]

    def beside_third():
        for j in range(3):
            spread(0, j, y_2[0, 0][j] * root)
        sum_finish(1, flight.pop(1))
        flight[2] = sum_start(2)

    product = exchange(2, terms, True, beside_third)
    for j in range(3):
        spread(1, j, 2.0 * product[0, 0][j] * weight_sq[0, 0][j] * root - t_1[j])
    sum_finish(2, flight.pop(2))
    result_ref[...] = jnp.transpose(moments_ref[...])[0:4, :]


def on_device(
    sizes,
    displacements,
    species,
    neighbor_index,
    probes,
    embedding,
    w_radial1,
    w_radial2,
    w_node,
    readout,
    spectral_radius,
):
    vmem = pl.BlockSpec(memory_space=pltpu.VMEM)
    most = max(sizes)
    operands = (
        displacements.reshape(3, 4, 32),
        species.reshape(-1, 32),
        neighbor_index.reshape(-1, 32),
        probes.reshape(-1, 32),
        embedding,
        w_radial1,
        w_radial2,
        w_node,
        readout.reshape(1, -1),
    )
    cheb, result = pl.pallas_call(
        functools.partial(kernel, sizes),
        out_shape=(
            jax.ShapeDtypeStruct((24 * PROBES, 32), F32),
            jax.ShapeDtypeStruct((4, PROBES), F32),
        ),
        in_specs=[pl.BlockSpec(memory_space=pltpu.SMEM)] + [pl.BlockSpec(memory_space=pl.ANY)] * 9,
        out_specs=(vmem, vmem),
        scratch_shapes=[
            pltpu.VMEM((8, LANES), F32),
            pltpu.VMEM((3, 32, LANES), F32),
            pltpu.VMEM((3, 2, 32, LANES), F32),
            pltpu.VMEM((3, 48, LANES), F32),
            pltpu.VMEM((3, 2, 48, LANES), F32),
            pltpu.VMEM((3, 26, 64, LANES), F32),
            pltpu.VMEM((3, 26, 64, LANES), F32),
            pltpu.VMEM((3, 8, LANES), F32),
            pltpu.VMEM((3, most, 8, LANES), F32),
            pltpu.SemaphoreType.DMA((2, 6)),
            pltpu.SemaphoreType.DMA((2, 6)),
            pltpu.SemaphoreType.DMA((3, 2, 26)),
            pltpu.SemaphoreType.DMA((3, 2, most)),
            pltpu.VMEM((8 * NC, LANES), F32),
            pltpu.VMEM((24 * NC, LANES), F32),
            pltpu.VMEM((11, 32, LANES), F32),
            pltpu.VMEM((3 * HID, LANES), F32),
            pltpu.VMEM((NC, 128, LANES), F32),
            pltpu.VMEM((NC, HID, LANES), F32),
            pltpu.VMEM((2, 128, LANES), F32),
            pltpu.VMEM((NC * NC, 8, LANES), F32),
            pltpu.VMEM((3 * NC, 8, LANES), F32),
            pltpu.VMEM((NC, 8, LANES), F32),
            pltpu.VMEM((3 * NC, 8, LANES), F32),
            pltpu.VMEM((8, LANES), F32),
            pltpu.VMEM((8, LANES), F32),
        ]
        + [pltpu.VMEM(v.shape, v.dtype) for v in operands]
        + [pltpu.SemaphoreType.DMA((len(operands),))],
        compiler_params=pltpu.CompilerParams(
            collective_id=0, has_side_effects=True, vmem_limit_bytes=60 * 2**20
        ),
        name="chebyshev",
    )(
        spectral_radius,
        *operands,
    )
    return cheb.reshape((2,) + probes.shape), result


def solution(mesh):
    placed = (
        P(None, "gx", "gy", "gz"),
        P("gx", "gy", "gz"),
        P(None, "gx", "gy", "gz"),
        P(None, None, "gx", "gy", "gz"),
        P(),
        P(),
        P(),
        P(),
        P(),
        P(),
    )
    return jax.shard_map(
        functools.partial(on_device, tuple(mesh.shape[axis] for axis in AXES)),
        mesh=mesh,
        in_specs=placed,
        out_specs=(P(None, None, None, "gx", "gy", "gz"), P()),
        check_vma=False,
    )
```

```python
import functools
import math

import jax
import jax.numpy as jnp
from jax import lax
from jax.experimental import pallas as pl
from jax.experimental.pallas import tpu as pltpu
from jax.sharding import PartitionSpec as P

SPACING = 2.2
CUTOFF = 5.0
NORM_SCALE = 0.22360679774997896
MASSES = (28.0855, 15.999, 22.99)
HIGHEST = lax.Precision.HIGHEST
MESH = pl.DeviceIdType.MESH
F32 = jnp.float32
BF16 = jnp.bfloat16

CODES = tuple(sorted((c for c in range(27) if c != 13), key=lambda c: (c % 3 != 1, c)))
ORDER = {c: n for n, c in enumerate(CODES)}
NC = len(CODES)
FLAT = 8
WAYS = tuple(
    sorted(
        (
            (x, y, z)
            for x in (-1, 0, 1)
            for y in (-1, 0, 1)
            for z in (-1, 0, 1)
            if (x, y, z) != (0, 0, 0)
        ),
        key=lambda way: (way[2] == 0, -sum(map(abs, way))),
    )
)
BLOCKS = ((0, 7), (7, 14), (14, 20), (20, 26))
AXES = ("gx", "gy", "gz")
LANES = 128
HID = 64
PROBES = 8


def roll(value, by):
    return pltpu.roll(value, by % LANES, 1)


def high_low(value):
    high = value.astype(BF16).astype(F32)
    return high, value - high


def by_species(species, values):
    return jnp.where(species < 0.5, values[0], jnp.where(species < 1.5, values[1], values[2]))


def sin_cos(angle):
    off = angle - math.pi / 2
    square = off * off
    odd = jnp.full_like(off, -1.0 / math.factorial(15))
    for power in (13, 11, 9, 7, 5, 3, 1):
        odd = odd * square + (-1.0) ** (power // 2) / math.factorial(power)
    even = jnp.full_like(off, 1.0 / math.factorial(16))
    for power in (14, 12, 10, 8, 6, 4, 2, 0):
        even = even * square + (-1.0) ** (power // 2) / math.factorial(power)
    return even, -odd * off


class Lanes:
    def __init__(self):
        lane = lax.broadcasted_iota(jnp.int32, (8, LANES), 1)
        self.lane = lane
        self.upper = (lane >= 64, (lane & 32) != 0)
        self.z = lane & 31
        self.low_z = self.z < 16
        self.outer = (self.z < 3) | (self.z > 28)
        self.first = [self.z == j for j in range(3)]
        self.last = [self.z == 31 - j for j in range(3)]

    def swap(self, axis, value):
        if axis == 0:
            return roll(value, 64)
        return jnp.where(self.upper[1], roll(value, 32), roll(value, -32))

    def merge(self, axis, low_value, high_value):
        if axis < 2:
            return jnp.where(self.upper[axis], high_value, low_value)
        return jnp.where(self.low_z, low_value, high_value)

    def ends(self, low_values, high_values):
        out = jnp.zeros((8, LANES), F32)
        for j, (low, high) in enumerate(zip(low_values, high_values)):
            out = jnp.where(self.first[j], low, jnp.where(self.last[j], high, out))
        return out

    def pack(self, values):
        return self.ends(
            [roll(v, j) if j else v for j, v in enumerate(values)],
            [roll(v, -j) if j else v for j, v in enumerate(values)],
        )

    def unpack(self, packed, count):
        out = []
        for j in range(count):
            low, high = (roll(packed, -j), roll(packed, j)) if j else (packed, packed)
            out.append(jnp.where(self.first[0], low, jnp.where(self.last[0], high, 0.0)))
        return out


SITES = tuple((gx, gy) for gx in (0, 1) for gy in (0, 1))


def gather(lanes, ext, flat_only=False):
    count = len(ext[0, 0]) - 1
    along_x = {}
    for gy in (0, 1):
        own, ghost = ext[0, gy], ext[1, gy]
        along_x[0, gy] = own
        along_x[1, gy] = [lanes.swap(0, lanes.merge(0, g, o)) for o, g in zip(own, ghost)]
        along_x[-1, gy] = [lanes.swap(0, lanes.merge(0, o, g)) for o, g in zip(own, ghost)]
    out = {}
    for sx in (-1, 0, 1):
        own, ghost = along_x[sx, 0], along_x[sx, 1]
        along_y = {
            0: own,
            1: [lanes.swap(1, lanes.merge(1, g, o)) for o, g in zip(own, ghost)],
            -1: [lanes.swap(1, lanes.merge(1, o, g)) for o, g in zip(own, ghost)],
        }
        for sy in (-1, 0, 1):
            values, packed = along_y[sy][:count], along_y[sy][count]
            base = (sx + 1) * 9 + (sy + 1) * 3 + 1
            out[base] = values
            if flat_only:
                continue
            out[base + 1] = [
                jnp.where(lanes.last[0], roll(packed, 31 - j), roll(v, -1))
                for j, v in enumerate(values)
            ]
            out[base - 1] = [
                jnp.where(lanes.first[0], roll(packed, j - 31), roll(v, 1))
                for j, v in enumerate(values)
            ]
    return out


def scatter(lanes, edges):
    along_z = {}
    for sx in (-1, 0, 1):
        for sy in (-1, 0, 1):
            base = (sx + 1) * 9 + (sy + 1) * 3 + 1
            values, lows, highs = [], [], []
            for j in range(3):
                up, down = edges(base + 1, j), edges(base - 1, j)
                own = edges(base, j)
                own = own + jnp.where(lanes.first[0], 0.0, roll(up, 1))
                values.append(own + jnp.where(lanes.last[0], 0.0, roll(down, -1)))
                lows.append(roll(up, j - 31))
                highs.append(roll(down, 31 - j))
            along_z[sx, sy] = values + [lanes.ends(lows, highs)]
    along_y = {}
    for sx in (-1, 0, 1):
        items = list(zip(along_z[sx, -1], along_z[sx, 0], along_z[sx, 1]))
        along_y[sx, 0] = [m + lanes.swap(1, lanes.merge(1, up, down)) for down, m, up in items]
        along_y[sx, 1] = [lanes.swap(1, lanes.merge(1, down, up)) for down, m, up in items]
    ext = {}
    for gy in (0, 1):
        items = list(zip(along_y[-1, gy], along_y[0, gy], along_y[1, gy]))
        ext[0, gy] = [m + lanes.swap(0, lanes.merge(0, up, down)) for down, m, up in items]
        ext[1, gy] = [lanes.swap(0, lanes.merge(0, down, up)) for down, m, up in items]
    return ext


def kernel(
    sizes,
    radius_ref,
    *refs,
):
    sources, refs = refs[:9], refs[9:]
    (
        cheb_ref,
        result_ref,
        moments_ref,
        geo_send,
        geo_recv,
        halo_send,
        halo_recv,
        fold_send,
        fold_recv,
        sum_send,
        sum_recv,
        geo_sems,
        halo_sems,
        fold_sems,
        sum_sems,
        geo_ref,
        trig_ref,
        rows_ref,
        acc_ref,
        prod_ref,
        second_ref,
        node_ref,
        matrix_ref,
        dv_ref,
        dr_ref,
        edge_ref,
        small_ref,
        node_change_ref,
        total_ref,
        pack_ref,
    ) = refs[: -10]
    fetched, fetch_sems = refs[-10:-1], refs[-1]
    disp_ref, species_ref, index_ref, probes_ref, emb_ref, w1_ref, w2_ref, wn_ref, readout_ref = fetched
    fetches = [
        pltpu.make_async_copy(src, dst, fetch_sems.at[n])
        for n, (src, dst) in enumerate(zip(sources, fetched))
    ]
    for n in (0, 1, 3, 4, 5, 6, 7, 8, 2):
        fetches[n].start()

    place = [lax.axis_index(axis) for axis in AXES]

    def partner(axis, by):
        return lax.rem(place[axis] + (by + sizes[axis]), sizes[axis])

    barrier = pltpu.get_barrier_semaphore()
    partners = [(axis, by) for axis in range(3) for by in range(1, sizes[axis])]
    for axis, by in partners:
        pl.semaphore_signal(
            barrier, inc=1, device_id={AXES[axis]: partner(axis, by)}, device_id_type=MESH
        )

    def flat(ref, first, count, stride):
        return jnp.concatenate(
            [ref[pl.ds(first + q, count, stride=stride), :] for q in range(4)], axis=1
        )

    lanes = Lanes()
    pack_ref[0:8, :] = jnp.zeros((8, LANES), F32)
    for n in (0, 1):
        fetches[n].wait()
    pack_ref[0:3, :] = jnp.concatenate([disp_ref[:, q, :] for q in range(4)], axis=1)
    pack_ref[3:4, :] = jnp.concatenate(
        [species_ref[q : q + 1, :] for q in range(4)], axis=1
    ).astype(F32)
    for n in (3,):
        fetches[n].wait()
    species = pack_ref[3:4, :]
    inv_root = by_species(species, [1.0 / math.sqrt(m) for m in MASSES])
    root = by_species(species, [math.sqrt(m) for m in MASSES])
    probes = [flat(probes_ref, 4 * j, PROBES, 12) for j in range(3)]
    start = [p * inv_root for p in probes]

    pl.semaphore_wait(barrier, len(partners))

    def copy(src, dst, sems, number, axis, by):
        return pltpu.make_async_remote_copy(
            src_ref=src,
            dst_ref=dst,
            send_sem=sems.at[0, number],
            recv_sem=sems.at[1, number],
            device_id={AXES[axis]: partner(axis, by)},
            device_id_type=MESH,
        )

    def tile(n):
        return pl.ds(8 * n, 8)

    def halo_start(send, recv, sems, axis, arrays):
        for n, value in enumerate(arrays):
            send[axis, tile(n), :] = value
        rows = pl.ds(0, 8 * len(arrays))
        copies = [
            copy(send.at[axis, rows], recv.at[axis, d, rows], sems, 2 * axis + d, axis, 1 - 2 * d)
            for d in (0, 1)
        ]
        for c in copies:
            c.start()
        return copies

    def halo_finish(recv, axis, copies, count):
        for c in copies:
            c.wait()
        return [
            lanes.merge(axis, recv[axis, 1, tile(n), :], recv[axis, 0, tile(n), :])
            for n in range(count)
        ]

    geometry = {(0, 0): [pack_ref[0:8, :]]}
    geo = (geo_send, geo_recv, geo_sems)
    halo = (halo_send, halo_recv, halo_sems)
    copies = halo_start(*geo, 1, geometry[0, 0])
    halo_copies = halo_start(*halo, 1, start)

    for n in (4, 5, 6, 7, 8, 2):
        fetches[n].wait()
    for s in range(3):
        acc_ref[pl.ds(64 * s, 64), :] = w2_ref[...] * emb_ref[s : s + 1, :]
    to_node = jnp.dot(
        acc_ref[...], wn_ref[...], precision=HIGHEST, preferred_element_type=F32
    ) * NORM_SCALE
    flipped = [jnp.transpose(to_node[64 * s : 64 * s + 64, :]) for s in range(3)]
    flip = [high_low(f) for f in flipped]
    left_node = jnp.concatenate(
        [jnp.concatenate([hi, hi, lo], axis=1) for hi, lo in flip], axis=0
    ).astype(BF16)
    first_high, first_low = high_low(w1_ref[...] * math.sqrt(2.0 / CUTOFF))
    left_radial = jnp.transpose(
        jnp.concatenate([first_high, first_high, first_low, jnp.zeros_like(first_high)], axis=0)
    ).astype(BF16)
    small_ref[0:8, :] = jnp.zeros((8, LANES), F32)
    small_ref[0:3, :] = emb_ref[...]
    small_ref[3:4, :] = readout_ref[...]
    columns = jnp.transpose(small_ref[0:8, :])
    readout = columns[:, 3:4]

    row_lane = lax.broadcasted_iota(jnp.int32, (32, LANES), 1)
    home = (
        ((row_lane >> 6) + 1) * (4 * 34) + (((row_lane >> 5) & 1) + 1) * 34 + (row_lane & 31) + 1
    )
    off = flat(index_ref, 0, 32, 4) - home

    def unit(value, bound):
        return jnp.where(value > bound, 1, 0) - jnp.where(value < -bound, 1, 0)

    off_x = unit(off, 68)
    rest = off - 136 * off_x
    off_y = unit(rest, 17)
    off_z = rest - 34 * off_y
    code = (off_x + 1) * 9 + (off_y + 1) * 3 + off_z + 1
    bits = jnp.where(off == 0, 0, jnp.left_shift(jnp.ones_like(code), code))
    bits = jnp.sum(bits, axis=0, keepdims=True)

    geometry[0, 1] = halo_finish(geo_recv, 1, copies, 1)
    copies = halo_start(*geo, 0, geometry[0, 0] + geometry[0, 1])
    y_old = {(0, 0): start}
    y_old[0, 1] = halo_finish(halo_recv, 1, halo_copies, 3)
    ghosts = halo_finish(geo_recv, 0, copies, 2)
    geometry[1, 0], geometry[1, 1] = [ghosts[0]], [ghosts[1]]
    copies = halo_start(*geo, 2, [geometry[k][0] for k in SITES])
    halo_copies = halo_start(*halo, 0, y_old[0, 0] + y_old[0, 1])

    for n, c in enumerate(CODES):
        rows_ref[9, pl.ds(n, 1), :] = (jnp.right_shift(bits, c) & 1).astype(F32)

    def edges_of(seen, count):
        for n in range(count):
            geo_ref[tile(n), :] = seen[CODES[n]][0]
        code_row = lax.broadcasted_iota(jnp.int32, (count, LANES), 0)
        if count == FLAT:
            number = code_row + jnp.where(code_row >= 4, 1, 0)
            offs = (number // 3, number % 3, jnp.ones_like(number))
        else:
            number = code_row + jnp.where(code_row >= 4, 1, 0)
            pair = (code_row - FLAT) // 2
            flat = code_row < FLAT
            offs = (
                jnp.where(flat, number // 3, pair // 3),
                jnp.where(flat, number % 3, pair % 3),
                jnp.where(flat, 1, 2 * (code_row % 2)),
            )
        vectors = [
            (off - 1).astype(F32) * SPACING
            + geo_ref[pl.ds(j, count, stride=8), :]
            - pack_ref[j : j + 1, :]
            for j, off in enumerate(offs)
        ]
        filled = rows_ref[9, 0:count, :]
        present = filled > 0.5
        square = vectors[0] * vectors[0] + vectors[1] * vectors[1] + vectors[2] * vectors[2]
        distance = jnp.sqrt(jnp.where(present, square, 1.0))
        inverse = 1.0 / distance
        part = distance * (1.0 / CUTOFF)
        part_sq = part * part
        for j in range(3):
            rows_ref[j, 0:count, :] = vectors[j] * inverse
        rows_ref[3, 0:count, :] = inverse
        rows_ref[4, 0:count, :] = filled * (1.0 - part_sq) * (1.0 - part_sq)
        rows_ref[5, 0:count, :] = filled * (-4.0 / CUTOFF) * part * (1.0 - part_sq)
        rows_ref[6, 0:count, :] = filled * (-4.0 / CUTOFF**2) * (1.0 - 3.0 * part_sq)
        rows_ref[7, 0:count, :] = geo_ref[pl.ds(3, count, stride=8), :]
        sin_1, cos_1 = sin_cos(distance * (math.pi / CUTOFF))
        sin_k, cos_k = sin_1, cos_1
        sin_b, cos_b = jnp.zeros_like(sin_1), jnp.ones_like(cos_1)
        for k in range(8):
            omega = (k + 1) * math.pi / CUTOFF
            trig_ref[pl.ds(k, count, stride=24), :] = sin_k
            trig_ref[pl.ds(8 + k, count, stride=24), :] = cos_k * omega
            trig_ref[pl.ds(16 + k, count, stride=24), :] = sin_k * (-omega * omega)
            sin_k, sin_b = 2.0 * cos_1 * sin_k - sin_b, sin_k
            cos_k, cos_b = 2.0 * cos_1 * cos_k - cos_b, cos_k

    edges_of(gather(lanes, {k: v + v for k, v in geometry.items()}, True), FLAT)

    acc_ref[...] = jnp.zeros_like(acc_ref)

    def radial(pair, carry):
        blocks = []
        for i in (0, 1):
            for g in range(3):
                hi, lo = high_low(trig_ref[pl.ds((2 * pair + i) * 24 + 8 * g, 8), :])
                blocks.append(jnp.concatenate([hi, lo, hi, jnp.zeros_like(hi)], axis=0))
        right = jnp.concatenate(blocks, axis=1).astype(BF16)
        waves = jnp.dot(left_radial, right, preferred_element_type=F32)
        rights = []
        for i in (0, 1):
            n = 2 * pair + i
            wave = [waves[:, 128 * (3 * i + g) : 128 * (3 * i + g + 1)] for g in range(3)]
            inv = rows_ref[3, pl.ds(n, 1), :]
            env = [rows_ref[4 + g, pl.ds(n, 1), :] for g in range(3)]
            kind = rows_ref[7, pl.ds(n, 1), :]
            x_0 = wave[0] * inv
            x_1 = (wave[1] - x_0) * inv
            x_2 = (wave[2] - 2.0 * x_1) * inv
            gate = 1.0 / (1.0 + jnp.exp(-x_0))
            shut = 1.0 - gate
            value = x_0 * gate
            slope = gate + value * shut
            bend = shut * (2.0 * gate + value * (1.0 - 2.0 * gate))
            r_1 = slope * x_1
            r_2 = bend * x_1 * x_1 + slope * x_2
            h_0 = value * env[0]
            h_1 = r_1 * env[0] + value * env[1]
            h_2 = r_2 * env[0] + 2.0 * r_1 * env[1] + value * env[2]
            second_ref[n] = h_2
            for s in range(3):
                one = jnp.where(jnp.abs(kind - s) < 0.5, 1.0, 0.0)
                acc_ref[pl.ds(64 * s, 64), :] += h_0 * one
            hi, lo = high_low(h_1)
            rights.append(jnp.concatenate([hi, lo, hi], axis=0).astype(BF16))
        product = jnp.dot(
            left_node, jnp.concatenate(rights, axis=1), preferred_element_type=F32
        )
        for i in (0, 1):
            n = 2 * pair + i
            kind = rows_ref[7, pl.ds(n, 1), :]
            cols = slice(128 * i, 128 * i + 128)
            prod_ref[n] = by_species(
                kind, [product[128 * s : 128 * s + 128, cols] for s in range(3)]
            )
        return carry

    lax.fori_loop(0, FLAT // 2, radial, 0, unroll=True)
    ghosts = halo_finish(geo_recv, 2, copies, 4)
    for n, k in enumerate(SITES):
        geometry[k] = geometry[k] + [ghosts[n]]
    edges_of(gather(lanes, geometry), NC)
    ghosts = halo_finish(halo_recv, 0, halo_copies, 6)
    y_old[1, 0], y_old[1, 1] = ghosts[:3], ghosts[3:]
    halo_copies = halo_start(*halo, 2, [lanes.pack(y_old[k]) for k in SITES])
    lax.fori_loop(FLAT // 2, NC // 2, radial, 0, unroll=True)

    home_kind = jnp.where(
        lax.broadcasted_iota(jnp.int32, (8, LANES), 0).astype(F32) == species, 1.0, 0.0
    )
    home_kind = jnp.where(lax.broadcasted_iota(jnp.int32, (8, LANES), 0) < 3, home_kind, 0.0)
    node = jnp.dot(columns, home_kind, precision=HIGHEST, preferred_element_type=F32)
    node = node + jnp.dot(
        jnp.concatenate(flipped, axis=1), acc_ref[...], precision=HIGHEST, preferred_element_type=F32
    )
    gate = 1.0 / (1.0 + jnp.exp(-node))
    shut = 1.0 - gate
    value = node * gate
    node_slope = readout * (gate + value * shut)
    node_ref[0] = node_slope
    node_ref[1] = readout * (shut * (2.0 * gate + value * (1.0 - 2.0 * gate)))
    acc_ref[...] = jnp.dot(to_node, node_slope, precision=HIGHEST, preferred_element_type=F32)

    def edge_terms(n, carry):
        mine = prod_ref[n]
        kind = rows_ref[7, pl.ds(n, 1), :]
        pull = jnp.sum(mine * node_ref[0], axis=0, keepdims=True) * rows_ref[3, pl.ds(n, 1), :]
        back = by_species(kind, [acc_ref[64 * s : 64 * s + 64, :] for s in range(3)])
        curve = jnp.sum(back * second_ref[n], axis=0, keepdims=True)
        rows_ref[8, pl.ds(n, 1), :] = pull
        rows_ref[10, pl.ds(n, 1), :] = curve - pull
        return carry

    lax.fori_loop(0, NC, edge_terms, 0, unroll=2)
    def matrices():
        for low, high in BLOCKS:

            def edge_matrix(n, carry, low=low, high=high):
                bent = prod_ref[n] * node_ref[1]
                for m in range(high):
                    both = jnp.sum(bent * prod_ref[m], axis=0, keepdims=True)
                    both = jnp.broadcast_to(both, (8, LANES))
                    matrix_ref[n * NC + m] = both
                    if m < low:
                        matrix_ref[m * NC + n] = both
                matrix_ref[n * NC + n] = matrix_ref[n * NC + n] + rows_ref[10, pl.ds(n, 1), :]
                return carry

            lax.fori_loop(low, high, edge_matrix, 0)

    ghosts = halo_finish(halo_recv, 2, halo_copies, 4)
    for n, k in enumerate(SITES):
        y_old[k] = y_old[k] + [ghosts[n]]
    scale = 1.0 / radius_ref[0]
    weight_sq = {}
    for k in SITES:
        own, ghost = [
            by_species(g[3:4, :], [1.0 / m for m in MASSES]) * scale + jnp.zeros((8, LANES), F32)
            for g in geometry[k]
        ]
        weight_sq[k] = [own] * 3 + [lanes.pack([ghost] * 3)]

    def local_product(y, through_node=False):
        views = gather(lanes, y)
        for n, c in enumerate(CODES):
            total = jnp.zeros((8, LANES), F32)
            for j in range(3):
                change = views[c][j] - views[13][j]
                dv_ref[3 * n + j] = change
                total = total + rows_ref[j, n : n + 1, :] * change
            dr_ref[n] = total

        if through_node:
            def one_probe(p, carry):
                for part in range(2):
                    half = pl.ds(64 * part, 64)
                    change = jnp.zeros((64, LANES), F32)
                    for n in range(NC):
                        change = change + prod_ref[n, half, :] * dr_ref[n, pl.ds(p, 1), :]
                    node_change_ref[half, :] = change * node_ref[1, half, :]
                for n in range(NC):
                    both = jnp.sum(prod_ref[n] * node_change_ref[...], axis=0, keepdims=True)
                    total_ref[n, pl.ds(p, 1), :] = both
                return carry

            lax.fori_loop(0, PROBES, one_probe, 0)

        def force(n, carry):
            if through_node:
                total = total_ref[n] + rows_ref[10, pl.ds(n, 1), :] * dr_ref[n]
            else:
                total = matrix_ref[n * NC] * dr_ref[0]
                for m in range(1, NC):
                    total = total + matrix_ref[n * NC + m] * dr_ref[m]
            pull = rows_ref[8, pl.ds(n, 1), :]
            out, work = [], carry[3]
            for j in range(3):
                change = dv_ref[3 * n + j]
                edge = rows_ref[j, pl.ds(n, 1), :] * total + pull * change
                edge_ref[3 * n + j] = edge
                out.append(carry[j] - edge)
                work = work + edge * change
            return tuple(out) + (work,)

        zero = jnp.zeros((8, LANES), F32)
        centre = lax.fori_loop(0, NC, force, (zero,) * 4, unroll=2)
        terms = scatter(
            lanes, lambda c, j: centre[j] if c == 13 else edge_ref[3 * ORDER[c] + j]
        )
        return terms, centre[3] * scale

    def exchange(number, held, own_only, beside):
        count = 3 if own_only else 4

        def leaving(axis, sign, table):
            out = {}
            for k, own in table.items():
                if sign == 0:
                    if k[axis] == 0 or not own_only:
                        out[k] = own
                elif k[axis] == 0:
                    ghost = table[(1, k[1]) if axis == 0 else (k[0], 1)]
                    pairs = zip(ghost, own) if sign > 0 else zip(own, ghost)
                    out[k] = [lanes.merge(axis, low, high) for low, high in pairs]
            return out

        def arriving(axis, plus, minus):
            out = {}
            for k in plus:
                out[k] = [lanes.merge(axis, p, m) for p, m in zip(plus[k], minus[k])]
                if not own_only:
                    other = (1, k[1]) if axis == 0 else (k[0], 1)
                    out[other] = [lanes.merge(axis, m, p) for p, m in zip(plus[k], minus[k])]
            return out

        def joined(first, *others):
            return {
                k: [sum(o[k][n] for o in others) + v for n, v in enumerate(items)]
                for k, items in first.items()
            }

        def pair(first, second):
            moved = lanes.merge(2, roll(second, 3), roll(second, -3))
            return jnp.where(lanes.outer, first, moved)

        def second_of(both):
            return lanes.merge(2, roll(both, -3), roll(both, 3))

        layers = {0: {k: v[:count] for k, v in held.items()}}
        for sign in (1, -1):
            layers[sign] = {}
            for k, v in held.items():
                own = lanes.pack(v[:3])
                low, high = (v[3], own) if sign > 0 else (own, v[3])
                layers[sign][k] = [lanes.merge(2, low, high)]

        copies, keys = {}, {}
        for slot, way in enumerate(WAYS):
            table = leaving(1, way[1], leaving(0, way[0], layers[way[2]]))
            keys[way] = sorted(table)
            items = [v for k in keys[way] for v in table[k]]
            if way[2] and len(items) > 1:
                items = [pair(*items[n : n + 2]) for n in range(0, len(items), 2)]
            for n, v in enumerate(items):
                fold_send[number, slot, tile(n), :] = v
            rows = pl.ds(0, 8 * len(items))
            copies[way] = pltpu.make_async_remote_copy(
                src_ref=fold_send.at[number, slot, rows],
                dst_ref=fold_recv.at[number, slot, rows],
                send_sem=fold_sems.at[number, 0, slot],
                recv_sem=fold_sems.at[number, 1, slot],
                device_id=tuple(partner(axis, way[axis]) for axis in range(3)),
                device_id_type=MESH,
            )
            copies[way].start()
        beside()

        def arrived(*way):
            slot = WAYS.index(way)
            copies[way].wait_recv()
            count_of = count if way[2] == 0 else 1
            total = count_of * len(keys[way])
            if way[2] and total > 1:
                items = []
                for n in range(total // 2):
                    both = fold_recv[number, slot, tile(n), :]
                    items += [both, second_of(both)]
            else:
                items = [fold_recv[number, slot, tile(n), :] for n in range(total)]
            return {
                k: items[count_of * n : count_of * n + count_of] for n, k in enumerate(keys[way])
            }

        def plane(layer, centre):
            along_x = arriving(0, arrived(1, 0, layer), arrived(-1, 0, layer))
            sides = [
                joined(
                    arrived(0, s, layer),
                    arriving(0, arrived(1, s, layer), arrived(-1, s, layer)),
                )
                for s in (1, -1)
            ]
            return joined(centre, along_x, arriving(1, *sides))

        sites = SITES[:1] if own_only else SITES
        flat = plane(0, {k: layers[0][k] for k in sites})
        above = plane(1, arrived(0, 0, 1))
        below = plane(-1, arrived(0, 0, -1))
        out = {}
        for k in sites:
            more = lanes.unpack(lanes.merge(2, above[k][0], below[k][0]), 3)
            out[k] = [h + t for h, t in zip(flat[k][:3], more)]
            if not own_only:
                out[k].append(flat[k][3] + lanes.merge(2, below[k][0], above[k][0]))
        for c in copies.values():
            c.wait_send()
        return out

    def sum_start(axis):
        sum_send[axis] = moments_ref[...]
        copies = []
        for by in range(1, sizes[axis]):
            c = copy(
                sum_send.at[axis],
                sum_recv.at[axis, by],
                sum_sems.at[axis],
                by,
                axis,
                by,
            )
            c.start()
            copies.append(c)
        return copies

    def sum_finish(axis, copies):
        for c in copies:
            c.wait()
        sum_recv[axis, 0] = sum_send[axis]
        total = jnp.zeros((8, LANES), F32)
        for index in range(sizes[axis]):
            slot = lax.rem(place[axis] + (sizes[axis] - index), sizes[axis])
            total = total + sum_recv[axis, slot]
        moments_ref[...] = total

    terms, work_1 = local_product(y_old, True)
    product = exchange(0, terms, False, matrices)
    y_1 = {k: [a * w for a, w in zip(product[k], weight_sq[k])] for k in SITES}
    t_1 = [y_1[0, 0][j] * root for j in range(3)]
    flight = {}

    def beside_second():
        square = sum(p * p for p in probes)
        parts = (
            square,
            work_1,
            2.0 * sum(t * t for t in t_1) - square,
            4.0 * work_2 - 3.0 * work_1,
        )
        packed = jnp.zeros((8, LANES), F32)
        for k in range(4):
            total = jnp.sum(parts[k], axis=1, keepdims=True)
            packed = jnp.where(lanes.lane == k, total, packed)
        moments_ref[...] = packed
        flight[0] = sum_start(0)

    terms, work_2 = local_product(y_1)
    product = exchange(1, terms, False, beside_second)
    y_2 = {
        k: [2.0 * a * w - o for a, w, o in zip(product[k], weight_sq[k], y_old[k])] for k in SITES
    }
    sum_finish(0, flight.pop(0))
    flight[1] = sum_start(1)
    terms, unused = local_product(y_2)

    def spread(which, j, value):
        for q in range(4):
            part = value if q == 0 else roll(value, -32 * q)
            cheb_ref[pl.ds(96 * which + 4 * j + q, PROBES, stride=12), :] = part[:, 0:32]

    def beside_third():
        for j in range(3):
            spread(0, j, y_2[0, 0][j] * root)
        sum_finish(1, flight.pop(1))
        flight[2] = sum_start(2)

    product = exchange(2, terms, True, beside_third)
    for j in range(3):
        spread(1, j, 2.0 * product[0, 0][j] * weight_sq[0, 0][j] * root - t_1[j])
    sum_finish(2, flight.pop(2))
    result_ref[...] = jnp.transpose(moments_ref[...])[0:4, :]


def on_device(
    sizes,
    displacements,
    species,
    neighbor_index,
    probes,
    embedding,
    w_radial1,
    w_radial2,
    w_node,
    readout,
    spectral_radius,
):
    vmem = pl.BlockSpec(memory_space=pltpu.VMEM)
    most = max(sizes)
    operands = (
        displacements.reshape(3, 4, 32),
        species.reshape(-1, 32),
        neighbor_index.reshape(-1, 32),
        probes.reshape(-1, 32),
        embedding,
        w_radial1,
        w_radial2,
        w_node,
        readout.reshape(1, -1),
    )
    cheb, result = pl.pallas_call(
        functools.partial(kernel, sizes),
        out_shape=(
            jax.ShapeDtypeStruct((24 * PROBES, 32), F32),
            jax.ShapeDtypeStruct((4, PROBES), F32),
        ),
        in_specs=[pl.BlockSpec(memory_space=pltpu.SMEM)] + [pl.BlockSpec(memory_space=pl.ANY)] * 9,
        out_specs=(vmem, vmem),
        scratch_shapes=[
            pltpu.VMEM((8, LANES), F32),
            pltpu.VMEM((3, 32, LANES), F32),
            pltpu.VMEM((3, 2, 32, LANES), F32),
            pltpu.VMEM((3, 48, LANES), F32),
            pltpu.VMEM((3, 2, 48, LANES), F32),
            pltpu.VMEM((3, 26, 64, LANES), F32),
            pltpu.VMEM((3, 26, 64, LANES), F32),
            pltpu.VMEM((3, 8, LANES), F32),
            pltpu.VMEM((3, most, 8, LANES), F32),
            pltpu.SemaphoreType.DMA((2, 6)),
            pltpu.SemaphoreType.DMA((2, 6)),
            pltpu.SemaphoreType.DMA((3, 2, 26)),
            pltpu.SemaphoreType.DMA((3, 2, most)),
            pltpu.VMEM((8 * NC, LANES), F32),
            pltpu.VMEM((24 * NC, LANES), F32),
            pltpu.VMEM((11, 32, LANES), F32),
            pltpu.VMEM((3 * HID, LANES), F32),
            pltpu.VMEM((NC, 128, LANES), F32),
            pltpu.VMEM((NC, HID, LANES), F32),
            pltpu.VMEM((2, 128, LANES), F32),
            pltpu.VMEM((NC * NC, 8, LANES), F32),
            pltpu.VMEM((3 * NC, 8, LANES), F32),
            pltpu.VMEM((NC, 8, LANES), F32),
            pltpu.VMEM((3 * NC, 8, LANES), F32),
            pltpu.VMEM((8, LANES), F32),
            pltpu.VMEM((128, LANES), F32),
            pltpu.VMEM((NC, 8, LANES), F32),
            pltpu.VMEM((8, LANES), F32),
        ]
        + [pltpu.VMEM(v.shape, v.dtype) for v in operands]
        + [pltpu.SemaphoreType.DMA((len(operands),))],
        compiler_params=pltpu.CompilerParams(
            collective_id=0, has_side_effects=True, vmem_limit_bytes=60 * 2**20
        ),
        name="chebyshev",
    )(
        spectral_radius,
        *operands,
    )
    return cheb.reshape((2,) + probes.shape), result


def solution(mesh):
    placed = (
        P(None, "gx", "gy", "gz"),
        P("gx", "gy", "gz"),
        P(None, "gx", "gy", "gz"),
        P(None, None, "gx", "gy", "gz"),
        P(),
        P(),
        P(),
        P(),
        P(),
        P(),
    )
    return jax.shard_map(
        functools.partial(on_device, tuple(mesh.shape[axis] for axis in AXES)),
        mesh=mesh,
        in_specs=placed,
        out_specs=(P(None, None, None, "gx", "gy", "gz"), P()),
        check_vma=False,
    )
```

```python
import functools
import math

import jax
import jax.numpy as jnp
from jax import lax
from jax.experimental import pallas as pl
from jax.experimental.pallas import tpu as pltpu
from jax.sharding import PartitionSpec as P

SPACING = 2.2
CUTOFF = 5.0
NORM_SCALE = 0.22360679774997896
MASSES = (28.0855, 15.999, 22.99)
HIGHEST = lax.Precision.HIGHEST
MESH = pl.DeviceIdType.MESH
F32 = jnp.float32
BF16 = jnp.bfloat16

CODES = tuple(sorted((c for c in range(27) if c != 13), key=lambda c: (c % 3 != 1, c)))
ORDER = {c: n for n, c in enumerate(CODES)}
NC = len(CODES)
FLAT = 8
WAYS = tuple(
    sorted(
        (
            (x, y, z)
            for x in (-1, 0, 1)
            for y in (-1, 0, 1)
            for z in (-1, 0, 1)
            if (x, y, z) != (0, 0, 0)
        ),
        key=lambda way: (way[2] == 0, -sum(map(abs, way))),
    )
)
BLOCKS = ((0, 7), (7, 14), (14, 20), (20, 26))
AXES = ("gx", "gy", "gz")
LANES = 128
HID = 64
PROBES = 8


def roll(value, by):
    return pltpu.roll(value, by % LANES, 1)


def high_low(value):
    high = value.astype(BF16).astype(F32)
    return high, value - high


def by_species(species, values):
    return jnp.where(species < 0.5, values[0], jnp.where(species < 1.5, values[1], values[2]))


def sin_cos(angle):
    off = angle - math.pi / 2
    square = off * off
    odd = jnp.full_like(off, -1.0 / math.factorial(15))
    for power in (13, 11, 9, 7, 5, 3, 1):
        odd = odd * square + (-1.0) ** (power // 2) / math.factorial(power)
    even = jnp.full_like(off, 1.0 / math.factorial(16))
    for power in (14, 12, 10, 8, 6, 4, 2, 0):
        even = even * square + (-1.0) ** (power // 2) / math.factorial(power)
    return even, -odd * off


class Lanes:
    def __init__(self):
        lane = lax.broadcasted_iota(jnp.int32, (8, LANES), 1)
        self.lane = lane
        self.upper = (lane >= 64, (lane & 32) != 0)
        self.z = lane & 31
        self.low_z = self.z < 16
        self.outer = (self.z < 3) | (self.z > 28)
        self.first = [self.z == j for j in range(3)]
        self.last = [self.z == 31 - j for j in range(3)]

    def swap(self, axis, value):
        if axis == 0:
            return roll(value, 64)
        return jnp.where(self.upper[1], roll(value, 32), roll(value, -32))

    def merge(self, axis, low_value, high_value):
        if axis < 2:
            return jnp.where(self.upper[axis], high_value, low_value)
        return jnp.where(self.low_z, low_value, high_value)

    def ends(self, low_values, high_values):
        out = jnp.zeros((8, LANES), F32)
        for j, (low, high) in enumerate(zip(low_values, high_values)):
            out = jnp.where(self.first[j], low, jnp.where(self.last[j], high, out))
        return out

    def pack(self, values):
        return self.ends(
            [roll(v, j) if j else v for j, v in enumerate(values)],
            [roll(v, -j) if j else v for j, v in enumerate(values)],
        )

    def unpack(self, packed, count):
        out = []
        for j in range(count):
            low, high = (roll(packed, -j), roll(packed, j)) if j else (packed, packed)
            out.append(jnp.where(self.first[0], low, jnp.where(self.last[0], high, 0.0)))
        return out


SITES = tuple((gx, gy) for gx in (0, 1) for gy in (0, 1))


def gather(lanes, ext, flat_only=False):
    count = len(ext[0, 0]) - 1
    along_x = {}
    for gy in (0, 1):
        own, ghost = ext[0, gy], ext[1, gy]
        along_x[0, gy] = own
        along_x[1, gy] = [lanes.swap(0, lanes.merge(0, g, o)) for o, g in zip(own, ghost)]
        along_x[-1, gy] = [lanes.swap(0, lanes.merge(0, o, g)) for o, g in zip(own, ghost)]
    out = {}
    for sx in (-1, 0, 1):
        own, ghost = along_x[sx, 0], along_x[sx, 1]
        along_y = {
            0: own,
            1: [lanes.swap(1, lanes.merge(1, g, o)) for o, g in zip(own, ghost)],
            -1: [lanes.swap(1, lanes.merge(1, o, g)) for o, g in zip(own, ghost)],
        }
        for sy in (-1, 0, 1):
            values, packed = along_y[sy][:count], along_y[sy][count]
            base = (sx + 1) * 9 + (sy + 1) * 3 + 1
            out[base] = values
            if flat_only:
                continue
            out[base + 1] = [
                jnp.where(lanes.last[0], roll(packed, 31 - j), roll(v, -1))
                for j, v in enumerate(values)
            ]
            out[base - 1] = [
                jnp.where(lanes.first[0], roll(packed, j - 31), roll(v, 1))
                for j, v in enumerate(values)
            ]
    return out


def scatter(lanes, edges):
    along_z = {}
    for sx in (-1, 0, 1):
        for sy in (-1, 0, 1):
            base = (sx + 1) * 9 + (sy + 1) * 3 + 1
            values, lows, highs = [], [], []
            for j in range(3):
                up, down = edges(base + 1, j), edges(base - 1, j)
                own = edges(base, j)
                own = own + jnp.where(lanes.first[0], 0.0, roll(up, 1))
                values.append(own + jnp.where(lanes.last[0], 0.0, roll(down, -1)))
                lows.append(roll(up, j - 31))
                highs.append(roll(down, 31 - j))
            along_z[sx, sy] = values + [lanes.ends(lows, highs)]
    along_y = {}
    for sx in (-1, 0, 1):
        items = list(zip(along_z[sx, -1], along_z[sx, 0], along_z[sx, 1]))
        along_y[sx, 0] = [m + lanes.swap(1, lanes.merge(1, up, down)) for down, m, up in items]
        along_y[sx, 1] = [lanes.swap(1, lanes.merge(1, down, up)) for down, m, up in items]
    ext = {}
    for gy in (0, 1):
        items = list(zip(along_y[-1, gy], along_y[0, gy], along_y[1, gy]))
        ext[0, gy] = [m + lanes.swap(0, lanes.merge(0, up, down)) for down, m, up in items]
        ext[1, gy] = [lanes.swap(0, lanes.merge(0, down, up)) for down, m, up in items]
    return ext


def kernel(
    sizes,
    radius_ref,
    *refs,
):
    sources, refs = refs[:9], refs[9:]
    (
        cheb_ref,
        result_ref,
        moments_ref,
        geo_send,
        geo_recv,
        halo_send,
        halo_recv,
        fold_send,
        fold_recv,
        sum_send,
        sum_recv,
        geo_sems,
        halo_sems,
        fold_sems,
        sum_sems,
        geo_ref,
        trig_ref,
        rows_ref,
        acc_ref,
        prod_ref,
        second_ref,
        node_ref,
        matrix_ref,
        dv_ref,
        dr_ref,
        edge_ref,
        small_ref,
        node_change_ref,
        total_ref,
        pack_ref,
    ) = refs[: -10]
    fetched, fetch_sems = refs[-10:-1], refs[-1]
    disp_ref, species_ref, index_ref, probes_ref, emb_ref, w1_ref, w2_ref, wn_ref, readout_ref = fetched
    fetches = [
        pltpu.make_async_copy(src, dst, fetch_sems.at[n])
        for n, (src, dst) in enumerate(zip(sources, fetched))
    ]
    for n in (0, 1, 3, 4, 5, 6, 7, 8, 2):
        fetches[n].start()

    place = [lax.axis_index(axis) for axis in AXES]

    def partner(axis, by):
        return lax.rem(place[axis] + (by + sizes[axis]), sizes[axis])

    barrier = pltpu.get_barrier_semaphore()
    partners = [(axis, by) for axis in range(3) for by in range(1, sizes[axis])]
    for axis, by in partners:
        pl.semaphore_signal(
            barrier, inc=1, device_id={AXES[axis]: partner(axis, by)}, device_id_type=MESH
        )

    def flat(ref, first, count, stride):
        return jnp.concatenate(
            [ref[pl.ds(first + q, count, stride=stride), :] for q in range(4)], axis=1
        )

    lanes = Lanes()
    pack_ref[0:8, :] = jnp.zeros((8, LANES), F32)
    for n in (0, 1):
        fetches[n].wait()
    pack_ref[0:3, :] = jnp.concatenate([disp_ref[:, q, :] for q in range(4)], axis=1)
    pack_ref[3:4, :] = jnp.concatenate(
        [species_ref[q : q + 1, :] for q in range(4)], axis=1
    ).astype(F32)
    for n in (3,):
        fetches[n].wait()
    species = pack_ref[3:4, :]
    inv_root = by_species(species, [1.0 / math.sqrt(m) for m in MASSES])
    root = by_species(species, [math.sqrt(m) for m in MASSES])
    probes = [flat(probes_ref, 4 * j, PROBES, 12) for j in range(3)]
    start = [p * inv_root for p in probes]

    pl.semaphore_wait(barrier, len(partners))

    def copy(src, dst, sems, number, axis, by):
        return pltpu.make_async_remote_copy(
            src_ref=src,
            dst_ref=dst,
            send_sem=sems.at[0, number],
            recv_sem=sems.at[1, number],
            device_id={AXES[axis]: partner(axis, by)},
            device_id_type=MESH,
        )

    def tile(n):
        return pl.ds(8 * n, 8)

    def halo_start(send, recv, sems, axis, arrays):
        for n, value in enumerate(arrays):
            send[axis, tile(n), :] = value
        rows = pl.ds(0, 8 * len(arrays))
        copies = [
            copy(send.at[axis, rows], recv.at[axis, d, rows], sems, 2 * axis + d, axis, 1 - 2 * d)
            for d in (0, 1)
        ]
        for c in copies:
            c.start()
        return copies

    def halo_finish(recv, axis, copies, count):
        for c in copies:
            c.wait()
        return [
            lanes.merge(axis, recv[axis, 1, tile(n), :], recv[axis, 0, tile(n), :])
            for n in range(count)
        ]

    geometry = {(0, 0): [pack_ref[0:8, :]]}
    geo = (geo_send, geo_recv, geo_sems)
    halo = (halo_send, halo_recv, halo_sems)
    copies = halo_start(*geo, 1, geometry[0, 0])
    halo_copies = halo_start(*halo, 1, start)

    for n in (4, 5, 6, 7, 8, 2):
        fetches[n].wait()
    for s in range(3):
        acc_ref[pl.ds(64 * s, 64), :] = w2_ref[...] * emb_ref[s : s + 1, :]
    to_node = jnp.dot(
        acc_ref[...], wn_ref[...], precision=HIGHEST, preferred_element_type=F32
    ) * NORM_SCALE
    flipped = [jnp.transpose(to_node[64 * s : 64 * s + 64, :]) for s in range(3)]
    flip = [high_low(f) for f in flipped]
    left_node = jnp.concatenate(
        [jnp.concatenate([hi, hi, lo], axis=1) for hi, lo in flip], axis=0
    ).astype(BF16)
    first_high, first_low = high_low(w1_ref[...] * math.sqrt(2.0 / CUTOFF))
    left_radial = jnp.transpose(
        jnp.concatenate([first_high, first_high, first_low, jnp.zeros_like(first_high)], axis=0)
    ).astype(BF16)
    small_ref[0:8, :] = jnp.zeros((8, LANES), F32)
    small_ref[0:3, :] = emb_ref[...]
    small_ref[3:4, :] = readout_ref[...]
    columns = jnp.transpose(small_ref[0:8, :])
    readout = columns[:, 3:4]

    row_lane = lax.broadcasted_iota(jnp.int32, (32, LANES), 1)
    home = (
        ((row_lane >> 6) + 1) * (4 * 34) + (((row_lane >> 5) & 1) + 1) * 34 + (row_lane & 31) + 1
    )
    off = flat(index_ref, 0, 32, 4) - home

    def unit(value, bound):
        return jnp.where(value > bound, 1, 0) - jnp.where(value < -bound, 1, 0)

    off_x = unit(off, 68)
    rest = off - 136 * off_x
    off_y = unit(rest, 17)
    off_z = rest - 34 * off_y
    code = (off_x + 1) * 9 + (off_y + 1) * 3 + off_z + 1
    bits = jnp.where(off == 0, 0, jnp.left_shift(jnp.ones_like(code), code))
    bits = jnp.sum(bits, axis=0, keepdims=True)

    geometry[0, 1] = halo_finish(geo_recv, 1, copies, 1)
    copies = halo_start(*geo, 0, geometry[0, 0] + geometry[0, 1])
    y_old = {(0, 0): start}
    y_old[0, 1] = halo_finish(halo_recv, 1, halo_copies, 3)
    ghosts = halo_finish(geo_recv, 0, copies, 2)
    geometry[1, 0], geometry[1, 1] = [ghosts[0]], [ghosts[1]]
    copies = halo_start(*geo, 2, [geometry[k][0] for k in SITES])
    halo_copies = halo_start(*halo, 0, y_old[0, 0] + y_old[0, 1])

    for n, c in enumerate(CODES):
        rows_ref[9, pl.ds(n, 1), :] = (jnp.right_shift(bits, c) & 1).astype(F32)

    def edges_of(seen, count):
        for n in range(count):
            geo_ref[tile(n), :] = seen[CODES[n]][0]
        code_row = lax.broadcasted_iota(jnp.int32, (count, LANES), 0)
        if count == FLAT:
            number = code_row + jnp.where(code_row >= 4, 1, 0)
            offs = (number // 3, number % 3, jnp.ones_like(number))
        else:
            number = code_row + jnp.where(code_row >= 4, 1, 0)
            pair = (code_row - FLAT) // 2
            flat = code_row < FLAT
            offs = (
                jnp.where(flat, number // 3, pair // 3),
                jnp.where(flat, number % 3, pair % 3),
                jnp.where(flat, 1, 2 * (code_row % 2)),
            )
        vectors = [
            (off - 1).astype(F32) * SPACING
            + geo_ref[pl.ds(j, count, stride=8), :]
            - pack_ref[j : j + 1, :]
            for j, off in enumerate(offs)
        ]
        filled = rows_ref[9, 0:count, :]
        present = filled > 0.5
        square = vectors[0] * vectors[0] + vectors[1] * vectors[1] + vectors[2] * vectors[2]
        distance = jnp.sqrt(jnp.where(present, square, 1.0))
        inverse = 1.0 / distance
        part = distance * (1.0 / CUTOFF)
        part_sq = part * part
        for j in range(3):
            rows_ref[j, 0:count, :] = vectors[j] * inverse
        rows_ref[3, 0:count, :] = inverse
        rows_ref[4, 0:count, :] = filled * (1.0 - part_sq) * (1.0 - part_sq)
        rows_ref[5, 0:count, :] = filled * (-4.0 / CUTOFF) * part * (1.0 - part_sq)
        rows_ref[6, 0:count, :] = filled * (-4.0 / CUTOFF**2) * (1.0 - 3.0 * part_sq)
        rows_ref[7, 0:count, :] = geo_ref[pl.ds(3, count, stride=8), :]
        sin_1, cos_1 = sin_cos(distance * (math.pi / CUTOFF))
        sin_k, cos_k = sin_1, cos_1
        sin_b, cos_b = jnp.zeros_like(sin_1), jnp.ones_like(cos_1)
        for k in range(8):
            omega = (k + 1) * math.pi / CUTOFF
            trig_ref[pl.ds(k, count, stride=24), :] = sin_k
            trig_ref[pl.ds(8 + k, count, stride=24), :] = cos_k * omega
            trig_ref[pl.ds(16 + k, count, stride=24), :] = sin_k * (-omega * omega)
            sin_k, sin_b = 2.0 * cos_1 * sin_k - sin_b, sin_k
            cos_k, cos_b = 2.0 * cos_1 * cos_k - cos_b, cos_k

    edges_of(gather(lanes, {k: v + v for k, v in geometry.items()}, True), FLAT)

    acc_ref[...] = jnp.zeros_like(acc_ref)

    def radial(pair, carry):
        blocks = []
        for i in (0, 1):
            for g in range(3):
                hi, lo = high_low(trig_ref[pl.ds((2 * pair + i) * 24 + 8 * g, 8), :])
                blocks.append(jnp.concatenate([hi, lo, hi, jnp.zeros_like(hi)], axis=0))
        right = jnp.concatenate(blocks, axis=1).astype(BF16)
        waves = jnp.dot(left_radial, right, preferred_element_type=F32)
        rights = []
        for i in (0, 1):
            n = 2 * pair + i
            wave = [waves[:, 128 * (3 * i + g) : 128 * (3 * i + g + 1)] for g in range(3)]
            inv = rows_ref[3, pl.ds(n, 1), :]
            env = [rows_ref[4 + g, pl.ds(n, 1), :] for g in range(3)]
            kind = rows_ref[7, pl.ds(n, 1), :]
            x_0 = wave[0] * inv
            x_1 = (wave[1] - x_0) * inv
            x_2 = (wave[2] - 2.0 * x_1) * inv
            gate = 1.0 / (1.0 + jnp.exp(-x_0))
            shut = 1.0 - gate
            value = x_0 * gate
            slope = gate + value * shut
            bend = shut * (2.0 * gate + value * (1.0 - 2.0 * gate))
            r_1 = slope * x_1
            r_2 = bend * x_1 * x_1 + slope * x_2
            h_0 = value * env[0]
            h_1 = r_1 * env[0] + value * env[1]
            h_2 = r_2 * env[0] + 2.0 * r_1 * env[1] + value * env[2]
            second_ref[n] = h_2
            for s in range(3):
                one = jnp.where(jnp.abs(kind - s) < 0.5, 1.0, 0.0)
                acc_ref[pl.ds(64 * s, 64), :] += h_0 * one
            hi, lo = high_low(h_1)
            rights.append(jnp.concatenate([hi, lo, hi], axis=0).astype(BF16))
        product = jnp.dot(
            left_node, jnp.concatenate(rights, axis=1), preferred_element_type=F32
        )
        for i in (0, 1):
            n = 2 * pair + i
            kind = rows_ref[7, pl.ds(n, 1), :]
            cols = slice(128 * i, 128 * i + 128)
            prod_ref[n] = by_species(
                kind, [product[128 * s : 128 * s + 128, cols] for s in range(3)]
            )
        return carry

    lax.fori_loop(0, FLAT // 2, radial, 0, unroll=True)
    ghosts = halo_finish(geo_recv, 2, copies, 4)
    for n, k in enumerate(SITES):
        geometry[k] = geometry[k] + [ghosts[n]]
    edges_of(gather(lanes, geometry), NC)
    ghosts = halo_finish(halo_recv, 0, halo_copies, 6)
    y_old[1, 0], y_old[1, 1] = ghosts[:3], ghosts[3:]
    halo_copies = halo_start(*halo, 2, [lanes.pack(y_old[k]) for k in SITES])
    lax.fori_loop(FLAT // 2, NC // 2, radial, 0, unroll=True)

    home_kind = jnp.where(
        lax.broadcasted_iota(jnp.int32, (8, LANES), 0).astype(F32) == species, 1.0, 0.0
    )
    home_kind = jnp.where(lax.broadcasted_iota(jnp.int32, (8, LANES), 0) < 3, home_kind, 0.0)
    node = jnp.dot(columns, home_kind, precision=HIGHEST, preferred_element_type=F32)
    node = node + jnp.dot(
        jnp.concatenate(flipped, axis=1), acc_ref[...], precision=HIGHEST, preferred_element_type=F32
    )
    gate = 1.0 / (1.0 + jnp.exp(-node))
    shut = 1.0 - gate
    value = node * gate
    node_slope = readout * (gate + value * shut)
    node_ref[0] = node_slope
    node_ref[1] = readout * (shut * (2.0 * gate + value * (1.0 - 2.0 * gate)))
    acc_ref[...] = jnp.dot(to_node, node_slope, precision=HIGHEST, preferred_element_type=F32)

    def edge_terms(n, carry):
        mine = prod_ref[n]
        kind = rows_ref[7, pl.ds(n, 1), :]
        pull = jnp.sum(mine * node_ref[0], axis=0, keepdims=True) * rows_ref[3, pl.ds(n, 1), :]
        back = by_species(kind, [acc_ref[64 * s : 64 * s + 64, :] for s in range(3)])
        curve = jnp.sum(back * second_ref[n], axis=0, keepdims=True)
        rows_ref[8, pl.ds(n, 1), :] = pull
        rows_ref[10, pl.ds(n, 1), :] = curve - pull
        return carry

    lax.fori_loop(0, NC, edge_terms, 0, unroll=2)
    def matrices():
        for low, high in BLOCKS:

            def edge_matrix(n, carry, low=low, high=high):
                bent = prod_ref[n] * node_ref[1]
                for m in range(high):
                    both = jnp.sum(bent * prod_ref[m], axis=0, keepdims=True)
                    both = jnp.broadcast_to(both, (8, LANES))
                    matrix_ref[n * NC + m] = both
                    if m < low:
                        matrix_ref[m * NC + n] = both
                matrix_ref[n * NC + n] = matrix_ref[n * NC + n] + rows_ref[10, pl.ds(n, 1), :]
                return carry

            lax.fori_loop(low, high, edge_matrix, 0)

    ghosts = halo_finish(halo_recv, 2, halo_copies, 4)
    for n, k in enumerate(SITES):
        y_old[k] = y_old[k] + [ghosts[n]]
    scale = 1.0 / radius_ref[0]
    weight_sq = {}
    for k in SITES:
        own, ghost = [
            by_species(g[3:4, :], [1.0 / m for m in MASSES]) * scale + jnp.zeros((8, LANES), F32)
            for g in geometry[k]
        ]
        weight_sq[k] = [own] * 3 + [lanes.pack([ghost] * 3)]

    def local_product(y, through_node=False):
        views = gather(lanes, y)
        for n, c in enumerate(CODES):
            total = jnp.zeros((8, LANES), F32)
            for j in range(3):
                change = views[c][j] - views[13][j]
                dv_ref[3 * n + j] = change
                total = total + rows_ref[j, n : n + 1, :] * change
            dr_ref[n] = total

        if through_node:
            def two_probes(step, carry):
                for part in range(2):
                    half = pl.ds(64 * part, 64)
                    change = [jnp.zeros((64, LANES), F32) for i in (0, 1)]
                    for n in range(NC):
                        mine = prod_ref[n, half, :]
                        for i in (0, 1):
                            change[i] = change[i] + mine * dr_ref[n, pl.ds(2 * step + i, 1), :]
                    for i in (0, 1):
                        node_change_ref[i, half, :] = change[i] * node_ref[1, half, :]
                for n in range(NC):
                    mine = prod_ref[n]
                    for i in (0, 1):
                        both = jnp.sum(mine * node_change_ref[i], axis=0, keepdims=True)
                        total_ref[n, pl.ds(2 * step + i, 1), :] = both
                return carry

            lax.fori_loop(0, PROBES // 2, two_probes, 0)

        def force(n, carry):
            if through_node:
                total = total_ref[n] + rows_ref[10, pl.ds(n, 1), :] * dr_ref[n]
            else:
                total = matrix_ref[n * NC] * dr_ref[0]
                for m in range(1, NC):
                    total = total + matrix_ref[n * NC + m] * dr_ref[m]
            pull = rows_ref[8, pl.ds(n, 1), :]
            out, work = [], carry[3]
            for j in range(3):
                change = dv_ref[3 * n + j]
                edge = rows_ref[j, pl.ds(n, 1), :] * total + pull * change
                edge_ref[3 * n + j] = edge
                out.append(carry[j] - edge)
                work = work + edge * change
            return tuple(out) + (work,)

        zero = jnp.zeros((8, LANES), F32)
        centre = lax.fori_loop(0, NC, force, (zero,) * 4, unroll=2)
        terms = scatter(
            lanes, lambda c, j: centre[j] if c == 13 else edge_ref[3 * ORDER[c] + j]
        )
        return terms, centre[3] * scale

    def exchange(number, held, own_only, beside):
        count = 3 if own_only else 4

        def leaving(axis, sign, table):
            out = {}
            for k, own in table.items():
                if sign == 0:
                    if k[axis] == 0 or not own_only:
                        out[k] = own
                elif k[axis] == 0:
                    ghost = table[(1, k[1]) if axis == 0 else (k[0], 1)]
                    pairs = zip(ghost, own) if sign > 0 else zip(own, ghost)
                    out[k] = [lanes.merge(axis, low, high) for low, high in pairs]
            return out

        def arriving(axis, plus, minus):
            out = {}
            for k in plus:
                out[k] = [lanes.merge(axis, p, m) for p, m in zip(plus[k], minus[k])]
                if not own_only:
                    other = (1, k[1]) if axis == 0 else (k[0], 1)
                    out[other] = [lanes.merge(axis, m, p) for p, m in zip(plus[k], minus[k])]
            return out

        def joined(first, *others):
            return {
                k: [sum(o[k][n] for o in others) + v for n, v in enumerate(items)]
                for k, items in first.items()
            }

        def pair(first, second):
            moved = lanes.merge(2, roll(second, 3), roll(second, -3))
            return jnp.where(lanes.outer, first, moved)

        def second_of(both):
            return lanes.merge(2, roll(both, -3), roll(both, 3))

        layers = {0: {k: v[:count] for k, v in held.items()}}
        for sign in (1, -1):
            layers[sign] = {}
            for k, v in held.items():
                own = lanes.pack(v[:3])
                low, high = (v[3], own) if sign > 0 else (own, v[3])
                layers[sign][k] = [lanes.merge(2, low, high)]

        copies, keys = {}, {}
        for slot, way in enumerate(WAYS):
            table = leaving(1, way[1], leaving(0, way[0], layers[way[2]]))
            keys[way] = sorted(table)
            items = [v for k in keys[way] for v in table[k]]
            if way[2] and len(items) > 1:
                items = [pair(*items[n : n + 2]) for n in range(0, len(items), 2)]
            for n, v in enumerate(items):
                fold_send[number, slot, tile(n), :] = v
            rows = pl.ds(0, 8 * len(items))
            copies[way] = pltpu.make_async_remote_copy(
                src_ref=fold_send.at[number, slot, rows],
                dst_ref=fold_recv.at[number, slot, rows],
                send_sem=fold_sems.at[number, 0, slot],
                recv_sem=fold_sems.at[number, 1, slot],
                device_id=tuple(partner(axis, way[axis]) for axis in range(3)),
                device_id_type=MESH,
            )
            copies[way].start()
        beside()

        def arrived(*way):
            slot = WAYS.index(way)
            copies[way].wait_recv()
            count_of = count if way[2] == 0 else 1
            total = count_of * len(keys[way])
            if way[2] and total > 1:
                items = []
                for n in range(total // 2):
                    both = fold_recv[number, slot, tile(n), :]
                    items += [both, second_of(both)]
            else:
                items = [fold_recv[number, slot, tile(n), :] for n in range(total)]
            return {
                k: items[count_of * n : count_of * n + count_of] for n, k in enumerate(keys[way])
            }

        def plane(layer, centre):
            along_x = arriving(0, arrived(1, 0, layer), arrived(-1, 0, layer))
            sides = [
                joined(
                    arrived(0, s, layer),
                    arriving(0, arrived(1, s, layer), arrived(-1, s, layer)),
                )
                for s in (1, -1)
            ]
            return joined(centre, along_x, arriving(1, *sides))

        sites = SITES[:1] if own_only else SITES
        flat = plane(0, {k: layers[0][k] for k in sites})
        above = plane(1, arrived(0, 0, 1))
        below = plane(-1, arrived(0, 0, -1))
        out = {}
        for k in sites:
            more = lanes.unpack(lanes.merge(2, above[k][0], below[k][0]), 3)
            out[k] = [h + t for h, t in zip(flat[k][:3], more)]
            if not own_only:
                out[k].append(flat[k][3] + lanes.merge(2, below[k][0], above[k][0]))
        for c in copies.values():
            c.wait_send()
        return out

    def sum_start(axis):
        sum_send[axis] = moments_ref[...]
        copies = []
        for by in range(1, sizes[axis]):
            c = copy(
                sum_send.at[axis],
                sum_recv.at[axis, by],
                sum_sems.at[axis],
                by,
                axis,
                by,
            )
            c.start()
            copies.append(c)
        return copies

    def sum_finish(axis, copies):
        for c in copies:
            c.wait()
        sum_recv[axis, 0] = sum_send[axis]
        total = jnp.zeros((8, LANES), F32)
        for index in range(sizes[axis]):
            slot = lax.rem(place[axis] + (sizes[axis] - index), sizes[axis])
            total = total + sum_recv[axis, slot]
        moments_ref[...] = total

    terms, work_1 = local_product(y_old, True)
    product = exchange(0, terms, False, matrices)
    y_1 = {k: [a * w for a, w in zip(product[k], weight_sq[k])] for k in SITES}
    t_1 = [y_1[0, 0][j] * root for j in range(3)]
    flight = {}

    def beside_second():
        square = sum(p * p for p in probes)
        parts = (
            square,
            work_1,
            2.0 * sum(t * t for t in t_1) - square,
            4.0 * work_2 - 3.0 * work_1,
        )
        packed = jnp.zeros((8, LANES), F32)
        for k in range(4):
            total = jnp.sum(parts[k], axis=1, keepdims=True)
            packed = jnp.where(lanes.lane == k, total, packed)
        moments_ref[...] = packed
        flight[0] = sum_start(0)

    terms, work_2 = local_product(y_1)
    product = exchange(1, terms, False, beside_second)
    y_2 = {
        k: [2.0 * a * w - o for a, w, o in zip(product[k], weight_sq[k], y_old[k])] for k in SITES
    }
    sum_finish(0, flight.pop(0))
    flight[1] = sum_start(1)
    terms, unused = local_product(y_2)

    def spread(which, j, value):
        for q in range(4):
            part = value if q == 0 else roll(value, -32 * q)
            cheb_ref[pl.ds(96 * which + 4 * j + q, PROBES, stride=12), :] = part[:, 0:32]

    def beside_third():
        for j in range(3):
            spread(0, j, y_2[0, 0][j] * root)
        sum_finish(1, flight.pop(1))
        flight[2] = sum_start(2)

    product = exchange(2, terms, True, beside_third)
    for j in range(3):
        spread(1, j, 2.0 * product[0, 0][j] * weight_sq[0, 0][j] * root - t_1[j])
    sum_finish(2, flight.pop(2))
    result_ref[...] = jnp.transpose(moments_ref[...])[0:4, :]


def on_device(
    sizes,
    displacements,
    species,
    neighbor_index,
    probes,
    embedding,
    w_radial1,
    w_radial2,
    w_node,
    readout,
    spectral_radius,
):
    vmem = pl.BlockSpec(memory_space=pltpu.VMEM)
    most = max(sizes)
    operands = (
        displacements.reshape(3, 4, 32),
        species.reshape(-1, 32),
        neighbor_index.reshape(-1, 32),
        probes.reshape(-1, 32),
        embedding,
        w_radial1,
        w_radial2,
        w_node,
        readout.reshape(1, -1),
    )
    cheb, result = pl.pallas_call(
        functools.partial(kernel, sizes),
        out_shape=(
            jax.ShapeDtypeStruct((24 * PROBES, 32), F32),
            jax.ShapeDtypeStruct((4, PROBES), F32),
        ),
        in_specs=[pl.BlockSpec(memory_space=pltpu.SMEM)] + [pl.BlockSpec(memory_space=pl.ANY)] * 9,
        out_specs=(vmem, vmem),
        scratch_shapes=[
            pltpu.VMEM((8, LANES), F32),
            pltpu.VMEM((3, 32, LANES), F32),
            pltpu.VMEM((3, 2, 32, LANES), F32),
            pltpu.VMEM((3, 48, LANES), F32),
            pltpu.VMEM((3, 2, 48, LANES), F32),
            pltpu.VMEM((3, 26, 64, LANES), F32),
            pltpu.VMEM((3, 26, 64, LANES), F32),
            pltpu.VMEM((3, 8, LANES), F32),
            pltpu.VMEM((3, most, 8, LANES), F32),
            pltpu.SemaphoreType.DMA((2, 6)),
            pltpu.SemaphoreType.DMA((2, 6)),
            pltpu.SemaphoreType.DMA((3, 2, 26)),
            pltpu.SemaphoreType.DMA((3, 2, most)),
            pltpu.VMEM((8 * NC, LANES), F32),
            pltpu.VMEM((24 * NC, LANES), F32),
            pltpu.VMEM((11, 32, LANES), F32),
            pltpu.VMEM((3 * HID, LANES), F32),
            pltpu.VMEM((NC, 128, LANES), F32),
            pltpu.VMEM((NC, HID, LANES), F32),
            pltpu.VMEM((2, 128, LANES), F32),
            pltpu.VMEM((NC * NC, 8, LANES), F32),
            pltpu.VMEM((3 * NC, 8, LANES), F32),
            pltpu.VMEM((NC, 8, LANES), F32),
            pltpu.VMEM((3 * NC, 8, LANES), F32),
            pltpu.VMEM((8, LANES), F32),
            pltpu.VMEM((2, 128, LANES), F32),
            pltpu.VMEM((NC, 8, LANES), F32),
            pltpu.VMEM((8, LANES), F32),
        ]
        + [pltpu.VMEM(v.shape, v.dtype) for v in operands]
        + [pltpu.SemaphoreType.DMA((len(operands),))],
        compiler_params=pltpu.CompilerParams(
            collective_id=0, has_side_effects=True, vmem_limit_bytes=60 * 2**20
        ),
        name="chebyshev",
    )(
        spectral_radius,
        *operands,
    )
    return cheb.reshape((2,) + probes.shape), result


def solution(mesh):
    placed = (
        P(None, "gx", "gy", "gz"),
        P("gx", "gy", "gz"),
        P(None, "gx", "gy", "gz"),
        P(None, None, "gx", "gy", "gz"),
        P(),
        P(),
        P(),
        P(),
        P(),
        P(),
    )
    return jax.shard_map(
        functools.partial(on_device, tuple(mesh.shape[axis] for axis in AXES)),
        mesh=mesh,
        in_specs=placed,
        out_specs=(P(None, None, None, "gx", "gy", "gz"), P()),
        check_vma=False,
    )
```
